512 devices in a mesh: req: 32 (over y, z_lo), head: 16 (over x, z_hi, core).
Axes of the slice: x: 4, y: 4, z: 16 (z_hi: 2, z_lo: 8; z = z_hi * 8 + z_lo), core: 2. Of those that a mesh axis runs over, the one named last changes fastest.
Arguments:
- hidden: bfloat16 [256, 2048], P('req', 'head'), may hold values from -6 to 6
- attn_gain: float32 [2048], replicated, may hold values from 0.1 to 1.9
- q_weight: bfloat16 [2048, 2048], P(None, 'head'), may hold values from -0.125 to 0.125
- gate_weight: bfloat16 [2048, 2048], P(None, 'head'), may hold values from -0.125 to 0.125
- key_value_weight: bfloat16 [2048, 2048], P(None, 'head'), may hold values from -0.125 to 0.125
- q_gain: float32 [128], replicated, may hold values from 0.5 to 1.5
- k_gain: float32 [128], replicated, may hold values from 0.5 to 2
- out_weight: bfloat16 [2048, 2048], P('head'), may hold values from -0.5 to 0.5
- prompt_key_cache: bfloat16 [32, 4096, 8, 128], P('req', 'head'), may hold values from -3.5 to 3.5
- prompt_value_cache: bfloat16 [32, 4096, 8, 128], P('req', 'head'), may hold values from -6 to 6
- tail_key_cache: bfloat16 [32, 4, 256, 8, 128], P('req', None, 'head'), may hold values from -3.5 to 3.5
- tail_value_cache: bfloat16 [32, 4, 256, 8, 128], P('req', None, 'head'), may hold values from -6 to 6
- mlp_gain: float32 [2048], replicated, may hold values from 0.1 to 1.9
- mlp_gate: bfloat16 [2048, 6144], P('req', 'head'), may hold values from -0.125 to 0.125
- mlp_up: bfloat16 [2048, 6144], P('req', 'head'), may hold values from -0.125 to 0.125
- mlp_down: bfloat16 [6144, 2048], P('head'), may hold values from -0.109375 to 0.109375
- final_gain: float32 [2048], P('head'), may hold values from 0.1 to 1.9
- score_weight: float32 [2048], P('head'), may hold values from -0.125 to 0.125
- prompt_lengths: int32 [32], replicated, may hold values from 1 to 4096, 65536 in all
- tail_lengths: int32 [32, 4], replicated, may hold values from 1 to 256, 512 in all within a row
- group_prompt: int32 [32], replicated, may hold values from 0 to 31, each once
Outputs:
- new_hidden: bfloat16 [256, 2048], P('req', 'head')
- score: float32 [256], P('req')
The draws below stay inside these ranges and needn't reach their ends.
Inputs may be any that keep to these rules, and one draw needn't show every extreme that they name: `group_prompt`: every prompt is held by exactly one group. `prompt_lengths`: one prompt has exactly 4096 prefix tokens. `tail_lengths`: in every prompt one continuation has exactly 256 tail tokens.
All inputs are finite; a program needn't handle non-finite values.
Results may differ from the reference program's by a relative error of at most 0.023.
Values may be sent and summed in bfloat16 or wider, within the bound.
A program may use at most 64 MiB of HBM per device.

```python
import math
import jax
import jax.numpy as jnp
import numpy as np
from jax import lax

MODEL_DIMENSION = 2048
QUERY_HEADS = 16
KEY_VALUE_HEADS = 8
HEAD_SIZE = 128
FF = 6144
PREFIX_SLOTS = 4096
TAIL_SLOTS = 256
CONTINUATION_COUNT = 4
NEW_TOKENS = 2
PROMPT_COUNT = 32
TOKENS = 256


def raised(values, key, source, target, blocks, factor):
    def block_of(axis_at):
        return (jnp.arange(values.shape[axis_at]) // (values.shape[axis_at] // blocks)).reshape((-1,) + (1,) * (values.ndim - 1 - axis_at))

    near = jax.random.permutation(key, blocks)[block_of(target)]
    second = (block_of(target) + blocks // 2) % blocks
    return jnp.where((block_of(source) == near) | (block_of(source) == second), factor * values, values)


def block_levels(rng, shape, split, smallest, largest):
    factor_of, own = 1.0, jax.random.fold_in(rng, 6)
    for dim, blocks in split:
        draws = jnp.exp(jax.random.uniform(jax.random.fold_in(own, dim), (blocks,), jnp.float32, smallest / len(split), largest / len(split)))
        factor_of = factor_of * jnp.repeat(draws, shape[dim] // blocks).reshape([-1 if axis == dim else 1 for axis in range(len(shape))])
    return factor_of


def profile(amount, total, most, skew):
    loads = [(1 << 20) // math.isqrt(rank ** skew) + 1 for rank in range(2, amount + 1)]
    surplus, holding = total - most - (amount - 1), [1] * (amount - 1)
    while surplus > 0:
        movable = [i for i in range(amount - 1) if holding[i] < most]
        pool, budget = sum([loads[i] for i in movable]), surplus
        for i in movable:
            more = min(most - holding[i], max(1, budget * loads[i] // pool), surplus)
            holding[i] = holding[i] + more
            surplus = surplus - more
    return np.array([most] + holding)


def ragged_sizes(rng, number_of, total, limit, skew):
    if number_of == 2:
        one = jax.random.randint(rng, (), max(1, total - limit), min(limit, total - 1) + 1)
        return jnp.stack([one, total - one])
    lengths = jnp.asarray(profile(number_of, total, limit, skew), jnp.int32)
    couples = (number_of - 1) // 2
    giver, sink = lengths[1:1 + 2 * couples:2], lengths[2:2 + 2 * couples:2]
    margin = jnp.minimum(giver - 1, limit - sink)
    moved = jax.random.randint(jax.random.fold_in(rng, 1), (couples,), 0, 1 << 20) % (margin + 1)
    lengths = lengths.at[1:1 + 2 * couples:2].set(giver - moved).at[2:2 + 2 * couples:2].set(sink + moved)
    return lengths[jax.random.permutation(jax.random.fold_in(rng, 2), number_of)]


def scatter_about(own_key, dims, width, limit, cuts=(), kind=jnp.bfloat16):
    array = width * jax.random.normal(own_key, dims, jnp.float32)
    if cuts:
        array = array * block_levels(own_key, dims, cuts, -0.22, 0.18)
    return jnp.clip(array, -limit, limit).astype(kind)


def noise_with(rng, extent, width, limit, shards, heavy, kind=jnp.bfloat16):
    values = width * jax.random.normal(rng, extent, jnp.float32)
    if shards:
        values = values * block_levels(rng, extent, shards, -0.22, 0.18)
    return jnp.clip(raised(values, jax.random.fold_in(rng, 3), *heavy), -limit, limit).astype(kind)


def setup_inputs(seed: int = 0) -> dict:
    key_of = jax.random.split(jax.random.key(seed), 22)
    return {
        "hidden": scatter_about(key_of[0], (TOKENS, MODEL_DIMENSION), 1.0, 6.0, ((0, 32), (1, 16))),
        "attn_gain": jnp.clip(1.0 + 0.18 * jax.random.normal(key_of[1], (MODEL_DIMENSION,), jnp.float32), 0.1, 1.9),
        "q_weight": scatter_about(key_of[2], (MODEL_DIMENSION, QUERY_HEADS * HEAD_SIZE), MODEL_DIMENSION ** -0.5, 0.125, ((1, 16),)),
        "gate_weight": scatter_about(key_of[3], (MODEL_DIMENSION, QUERY_HEADS * HEAD_SIZE), MODEL_DIMENSION ** -0.5, 0.125, ((1, 16),)),
        "key_value_weight": scatter_about(key_of[4], (MODEL_DIMENSION, 2 * KEY_VALUE_HEADS * HEAD_SIZE), MODEL_DIMENSION ** -0.5, 0.125, ((1, 16),)),
        "q_gain": jnp.clip(1.0 + 0.1 * jax.random.normal(key_of[5], (HEAD_SIZE,), jnp.float32), 0.5, 1.5),
        "k_gain": jnp.clip(jnp.exp(jax.random.uniform(key_of[6], (HEAD_SIZE,), jnp.float32, math.log(0.5), math.log(2.0))), 0.5, 2.0),
        "out_weight": scatter_about(key_of[7], (QUERY_HEADS * HEAD_SIZE, MODEL_DIMENSION), HEAD_SIZE ** -0.5, 0.5, ((0, 16),)),
        "prompt_key_cache": jnp.clip(jax.random.uniform(key_of[8], (PROMPT_COUNT, PREFIX_SLOTS, KEY_VALUE_HEADS, HEAD_SIZE), jnp.float32, -3.5, 3.5) * block_levels(key_of[8], (PROMPT_COUNT, PREFIX_SLOTS, KEY_VALUE_HEADS, HEAD_SIZE), ((0, 32), (1, 16)), -0.4, 0.0), -3.5, 3.5).astype(jnp.bfloat16),
        "prompt_value_cache": scatter_about(key_of[9], (PROMPT_COUNT, PREFIX_SLOTS, KEY_VALUE_HEADS, HEAD_SIZE), 1.0, 6.0, ((0, 32), (1, 16))),
        "tail_key_cache": jnp.clip(jax.random.uniform(key_of[10], (PROMPT_COUNT, CONTINUATION_COUNT, TAIL_SLOTS, KEY_VALUE_HEADS, HEAD_SIZE), jnp.float32, -3.5, 3.5) * block_levels(key_of[10], (PROMPT_COUNT, CONTINUATION_COUNT, TAIL_SLOTS, KEY_VALUE_HEADS, HEAD_SIZE), ((0, 32), (2, 16)), -0.4, 0.0), -3.5, 3.5).astype(jnp.bfloat16),
        "tail_value_cache": scatter_about(key_of[11], (PROMPT_COUNT, CONTINUATION_COUNT, TAIL_SLOTS, KEY_VALUE_HEADS, HEAD_SIZE), 1.0, 6.0, ((0, 32), (2, 16))),
        "mlp_gain": jnp.clip(1.0 + 0.18 * jax.random.normal(key_of[12], (MODEL_DIMENSION,), jnp.float32), 0.1, 1.9),
        "mlp_gate": scatter_about(key_of[13], (MODEL_DIMENSION, FF), MODEL_DIMENSION ** -0.5, 0.125, ((0, 32), (1, 16))),
        "mlp_up": scatter_about(key_of[14], (MODEL_DIMENSION, FF), MODEL_DIMENSION ** -0.5, 0.125, ((0, 32), (1, 16))),
        "mlp_down": noise_with(key_of[15], (FF, MODEL_DIMENSION), FF ** -0.5, 0.109375, ((0, 16),), (0, 1, 16, 2.0)),
        "final_gain": jnp.clip(1.0 + 0.18 * jax.random.normal(key_of[16], (MODEL_DIMENSION,), jnp.float32), 0.1, 1.9),
        "score_weight": scatter_about(key_of[17], (MODEL_DIMENSION,), MODEL_DIMENSION ** -0.5, 0.125, ((0, 16),), jnp.float32),
        "prompt_lengths": ragged_sizes(key_of[18], PROMPT_COUNT, PROMPT_COUNT * PREFIX_SLOTS // 2, PREFIX_SLOTS, 2).astype(jnp.int32),
        "tail_lengths": jax.vmap(lambda own: ragged_sizes(own, CONTINUATION_COUNT, CONTINUATION_COUNT * TAIL_SLOTS // 2, TAIL_SLOTS, 1))(jax.random.split(key_of[19], PROMPT_COUNT)).reshape((PROMPT_COUNT, CONTINUATION_COUNT)).astype(jnp.int32),
        "group_prompt": jax.random.permutation(key_of[20], PROMPT_COUNT).astype(jnp.int32),
    }


EPS = 1e-06
THETA = 1000000.0

def rms_scale(value, gain):
    return value * lax.rsqrt(lax.optimization_barrier(jnp.mean(value * value, axis=-1, keepdims=True)) + EPS) * gain

def rotate(value, position):
    head_width = value.shape[-1]
    half_width = head_width // 2
    frequency = jnp.exp(-math.log(THETA) * 2.0 * jnp.arange(half_width, dtype=jnp.float32) / head_width)
    angles = position.astype(jnp.float32)[:, None] * frequency[None, :]
    cosine = jnp.cos(angles)[:, None, :]
    sine_part = jnp.sin(angles)[:, None, :]
    first_half = value[..., :half_width]
    second_half = value[..., half_width:]
    return jnp.concatenate([first_half * cosine - second_half * sine_part, second_half * cosine + first_half * sine_part], axis=-1)

def rounded_values(value):
    return lax.optimization_barrier(value.astype(jnp.bfloat16)).astype(jnp.float32)

def reference(hidden, attn_gain, q_weight, gate_weight, key_value_weight, q_gain, k_gain, out_weight, prompt_key_cache, prompt_value_cache, tail_key_cache, tail_value_cache, mlp_gain, mlp_gate, mlp_up, mlp_down, final_gain, score_weight, prompt_lengths, tail_lengths, group_prompt):
    count_of_rows = CONTINUATION_COUNT * NEW_TOKENS
    sharing_count = QUERY_HEADS // KEY_VALUE_HEADS
    score_scale = 1.0 / math.sqrt(HEAD_SIZE)

    def one_group(group_id):
        prompt_id = group_prompt[group_id]
        prompt_len = prompt_lengths[prompt_id]
        tail_row = tail_lengths[prompt_id]
        position = (prompt_len + tail_row[:, None] + jnp.arange(NEW_TOKENS, dtype=jnp.int32)[None, :]).reshape(count_of_rows)
        block_rows = lax.dynamic_slice_in_dim(hidden, group_id * count_of_rows, count_of_rows, 0).astype(jnp.float32)
        normalized_hidden = rms_scale(block_rows, attn_gain).astype(jnp.bfloat16)
        gate_pre = jnp.dot(normalized_hidden, gate_weight, preferred_element_type=jnp.float32)
        query_rows = jnp.dot(normalized_hidden, q_weight, preferred_element_type=jnp.float32).reshape(count_of_rows, QUERY_HEADS, HEAD_SIZE)
        query_rows = rotate(rms_scale(query_rows, q_gain), position).astype(jnp.bfloat16)
        projected_rows = jnp.dot(normalized_hidden, key_value_weight, preferred_element_type=jnp.float32).reshape(count_of_rows, KEY_VALUE_HEADS, 2, HEAD_SIZE)
        incoming_keys = rotate(rms_scale(projected_rows[:, :, 0], k_gain), position).astype(jnp.bfloat16)
        incoming_values = projected_rows[:, :, 1].astype(jnp.bfloat16)
        query_groups = query_rows.astype(jnp.float32).reshape(count_of_rows, KEY_VALUE_HEADS, sharing_count, HEAD_SIZE)
        cache_keys = prompt_key_cache[group_id].astype(jnp.float32)
        cache_values = prompt_value_cache[group_id].astype(jnp.float32)
        scores = jnp.einsum('rkgd,tkd->rkgt', query_groups, cache_keys) * score_scale
        slot_live = jnp.arange(PREFIX_SLOTS, dtype=jnp.int32)[None, None, None, :] < prompt_len
        attention_weights = jnp.where(slot_live, jnp.exp(scores), 0.0)
        denominator = lax.optimization_barrier(jnp.sum(attention_weights, axis=-1))
        numerator = jnp.einsum('rkgt,tkd->rkgd', rounded_values(attention_weights), cache_values)
        continuation_rows = query_groups.reshape(CONTINUATION_COUNT, NEW_TOKENS, KEY_VALUE_HEADS, sharing_count, HEAD_SIZE)
        tkeys = tail_key_cache[group_id].astype(jnp.float32)
        tail_value_rows = tail_value_cache[group_id].astype(jnp.float32)
        scores = jnp.einsum('cjkgd,ctkd->cjkgt', continuation_rows, tkeys) * score_scale
        tail_live = jnp.arange(TAIL_SLOTS, dtype=jnp.int32)[None, :] < tail_row[:, None]
        attention_weights = jnp.where(tail_live[:, None, None, None, :], jnp.exp(scores), 0.0)
        denominator = denominator + lax.optimization_barrier(jnp.sum(attention_weights, axis=-1)).reshape(count_of_rows, KEY_VALUE_HEADS, sharing_count)
        numerator = numerator + jnp.einsum('ihbyw,iwbs->ihbys', rounded_values(attention_weights), tail_value_rows).reshape(count_of_rows, KEY_VALUE_HEADS, sharing_count, HEAD_SIZE)
        recent_key_rows = incoming_keys.astype(jnp.float32).reshape(CONTINUATION_COUNT, NEW_TOKENS, KEY_VALUE_HEADS, HEAD_SIZE)
        recent_value_rows = incoming_values.astype(jnp.float32).reshape(CONTINUATION_COUNT, NEW_TOKENS, KEY_VALUE_HEADS, HEAD_SIZE)
        scores = jnp.einsum('cjkgd,cukd->cjkgu', continuation_rows, recent_key_rows) * score_scale
        causal = jnp.arange(NEW_TOKENS, dtype=jnp.int32)[None, :] <= jnp.arange(NEW_TOKENS, dtype=jnp.int32)[:, None]
        attention_weights = jnp.where(causal[None, :, None, None, :], jnp.exp(scores), 0.0)
        denominator = denominator + lax.optimization_barrier(jnp.sum(attention_weights, axis=-1)).reshape(count_of_rows, KEY_VALUE_HEADS, sharing_count)
        numerator = numerator + jnp.einsum('bfmne,beml->bfmnl', rounded_values(attention_weights), recent_value_rows).reshape(count_of_rows, KEY_VALUE_HEADS, sharing_count, HEAD_SIZE)
        attention = (numerator / denominator[..., None]).reshape(count_of_rows, QUERY_HEADS * HEAD_SIZE)
        gated = (attention * jax.nn.sigmoid(gate_pre)).astype(jnp.bfloat16)
        return (block_rows + jnp.dot(gated, out_weight, preferred_element_type=jnp.float32)).astype(jnp.bfloat16)
    attended = lax.map(one_group, jnp.arange(PROMPT_COUNT, dtype=jnp.int32)).reshape(PROMPT_COUNT * count_of_rows, MODEL_DIMENSION)
    wide_rows = attended.astype(jnp.float32)
    mlp_in = rms_scale(wide_rows, mlp_gain).astype(jnp.bfloat16)
    gate_part = jnp.dot(mlp_in, mlp_gate, preferred_element_type=jnp.float32)
    up_part = jnp.dot(mlp_in, mlp_up, preferred_element_type=jnp.float32)
    act_rows = (jax.nn.silu(gate_part) * up_part).astype(jnp.bfloat16)
    result = (wide_rows + jnp.dot(act_rows, mlp_down, preferred_element_type=jnp.float32)).astype(jnp.bfloat16)
    owner_group = jnp.argsort(group_prompt).astype(jnp.int32)
    new_hidden = result.reshape(PROMPT_COUNT, count_of_rows, MODEL_DIMENSION)[owner_group].reshape(PROMPT_COUNT * count_of_rows, MODEL_DIMENSION)
    final_rows = new_hidden.astype(jnp.float32)
    score = lax.optimization_barrier(jnp.sum(final_rows * final_gain * score_weight, axis=-1)) * lax.rsqrt(lax.optimization_barrier(jnp.mean(final_rows * final_rows, axis=-1)) + EPS)
    return (new_hidden, score)
```

```python
import functools
import math

import jax
import jax.numpy as jnp
from jax import lax
from jax.experimental import pallas as pl
from jax.experimental.pallas import tpu as pltpu
from jax.sharding import PartitionSpec as P

EPS = 1e-06
THETA = 1000000.0
MESH = pl.DeviceIdType.MESH
BF = jnp.bfloat16
F32 = jnp.float32
WIDTH = 2048
SCALE = 1.0 / math.sqrt(128.0)

NEAR = [(2, 1), (2, 0), (1, 1), (3, 1), (1, 0), (3, 0), (0, 1)]
FAR = [(2, 1), (2, 0), (1, 1), (3, 1), (1, 0), (3, 0), (0, 1), (0, 0)]


def dot(a, b):
    return jnp.dot(a, b, preferred_element_type=F32)


def dot_nt(a, b):
    return lax.dot_general(a, b, (((1,), (1,)), ((), ())), preferred_element_type=F32)


def kernel(
    plen_ref, tlen_ref, gp_ref,
    hidden_ref, again_ref, qgain_ref, kgain_ref, mgain_ref, fgain_ref, sw_ref,
    wq_hbm, wg_hbm, wkv_hbm, wo_hbm, pk_hbm, pv_hbm, tk_hbm, tv_hbm, mg_hbm, mu_hbm, md_hbm,
    out_ref, score_ref,
    wq, wg, wkv, wo, kc, vc, wgate, wup, wdown,
    hb, hf, qs, qb, qf, fs, fb, mb, mf, nb, nf, sb, rb, tb, xb, ps, pb, ds_, db, ys, yb, zs, zb_, cs, cb, gs, gb,
    lsem, ssem, rsem,
):
    r = lax.axis_index("req")
    h = lax.axis_index("head")
    y, z = r // 8, r % 8
    x, zh, c = h // 4, (h // 2) % 2, h % 2
    zz, zb = z // 2, z % 2
    n = x * 2 + c
    oh = 1 - zh

    def head_at(dx, dz, dc):
        return ((x + dx) % 4) * 4 + ((zh + dz) % 2) * 2 + (c + dc) % 2

    def near_at(dx, dc):
        return ((x + dx) % 4) * 2 + (c + dc) % 2

    def send(src, dst, phase, at, dev):
        pltpu.make_async_remote_copy(
            src_ref=src, dst_ref=dst, send_sem=ssem.at[phase], recv_sem=rsem.at[at],
            device_id=dev, device_id_type=MESH,
        ).start()

    def waiter(ref, phase, at):
        return pltpu.make_async_remote_copy(
            src_ref=ref, dst_ref=ref, send_sem=ssem.at[phase], recv_sem=rsem.at[at],
            device_id=(r, head_at(0, 0, 1)), device_id_type=MESH,
        )

    def wait_recv(ref, at):
        waiter(ref, 0, at).wait_recv()

    def wait_send(ref, phase):
        waiter(ref, phase, 0).wait_send()

    own_w = y * 2 + zb
    local = [
        (mg_hbm, wgate.at[own_w]), (mu_hbm, wup.at[own_w]),
        (wq_hbm, wq), (wg_hbm, wg), (wkv_hbm, wkv),
        (pk_hbm, kc.at[pl.ds(0, 2048)]), (tk_hbm, kc.at[pl.ds(2048, 512)]),
        (pv_hbm, vc.at[pl.ds(0, 2048)]), (tv_hbm, vc.at[pl.ds(2048, 512)]),
        (wo_hbm, wo), (md_hbm, wdown),
    ]
    copies = [pltpu.make_async_copy(s, d, lsem.at[i]) for i, (s, d) in enumerate(local)]
    for cp in copies:
        cp.start()

    bar = pltpu.get_barrier_semaphore()

    def greet(dev):
        pl.semaphore_signal(bar, inc=1, device_id=dev, device_id_type=MESH)

    for dzl in range(1, 8):
        for dz in (1, 0):
            greet((y * 8 + (z + dzl) % 8, head_at(0, dz, 0)))
    for dzz in (2, 1, 3, 0):
        for dz in (1, 0):
            for dc in (1, 0):
                dev = (y * 8 + ((zz + dzz) % 4) * 2 + zb, zz * 4 + ((zh + dz) % 2) * 2 + (c + dc) % 2)
                if dzz == 0 and dz == 0 and dc == 0:
                    @pl.when(x != zz)
                    def _():
                        greet(dev)
                else:
                    greet(dev)
    for dx, dc in FAR:
        greet((r, head_at(dx, 1, dc)))
    for dx, dc in NEAR:
        greet((r, head_at(dx, 0, dc)))
    for dy in (2, 1, 3):
        for dzb in (1, 0):
            greet((((y + dy) % 4) * 8 + zz * 2 + (zb + dzb) % 2, h))

    hb[n] = hidden_ref[...]
    gs[...] = jnp.broadcast_to(fgain_ref[...] * sw_ref[...], (8, 128))

    prompt = gp_ref[r]
    plen = plen_ref[prompt]
    tails = [tlen_ref[prompt, i] for i in range(4)]

    def find(g, found):
        value = gp_ref[g]
        mine = jnp.where(value == r, g, found[8])
        return tuple(jnp.where(value == y * 8 + i, g, found[i]) for i in range(8)) + (mine,)

    owners = lax.fori_loop(0, 32, find, (jnp.int32(0),) * 9)

    row = lax.broadcasted_iota(jnp.int32, (8, 128), 0)
    lane = lax.broadcasted_iota(jnp.int32, (8, 128), 1)
    position = plen + row % 2
    for i in range(4):
        position = position + jnp.where(row // 2 == i, tails[i], 0)
    half_lane = (lane % 64).astype(F32)
    frequency = jnp.exp(-math.log(THETA) * 2.0 * half_lane / 128.0)
    angle = position.astype(F32) * frequency
    cosine = jnp.cos(angle)
    sine = jnp.sin(angle)
    sine = jnp.where(lane < 64, -sine, sine)

    def normed_rotated(value, gain):
        value = value * lax.rsqrt(jnp.mean(value * value, axis=-1, keepdims=True) + EPS) * gain
        return value * cosine + pltpu.roll(value, 64, 1) * sine

    pl.semaphore_wait(bar, 50 + jnp.where(x != zz, 1, 0))

    for dx, dc in FAR:
        send(hidden_ref, hf.at[n], 15, 1, (r, head_at(dx, 1, dc)))
    for dx, dc in NEAR:
        send(hidden_ref, hb.at[n], 0, 0, (r, head_at(dx, 0, dc)))
    send(gs, gb.at[zh], 11, 20, (r, head_at(0, 1, 0)))
    gb[zh] = gs[...]

    copies[0].wait()
    copies[1].wait()
    for dy in (2, 1, 3, 0):
        for dzb in (1, 0):
            if dy or dzb:
                dev = (((y + dy) % 4) * 8 + zz * 2 + (zb + dzb) % 2, h)
                send(wgate.at[own_w], wgate.at[own_w], 12, 21, dev)
                send(wup.at[own_w], wup.at[own_w], 13, 22, dev)

    for i in range(2, 11):
        copies[i].wait()

    def features(half, at):
        place = at * 4 + half * 2
        offset = pl.multiple_of(place * 128, 256)
        ref = hb if half is zh else hf
        value = jnp.concatenate([ref[at * 2].astype(F32), ref[at * 2 + 1].astype(F32)], axis=1)
        scaled = (value * again_ref[:, pl.ds(offset, 256)]).astype(BF)
        return value * value, scaled, offset

    wait_recv(hb.at[pl.ds(0, 7)], 0)
    squares = jnp.zeros((8, 256), F32)
    q_acc = jnp.zeros((8, 128), F32)
    g_acc = jnp.zeros((8, 128), F32)
    kv_acc = jnp.zeros((8, 128), F32)
    for i in range(4):
        square, scaled, offset = features(zh, i)
        squares = squares + square
        q_acc = q_acc + dot(scaled, wq[pl.ds(offset, 256), :])
        g_acc = g_acc + dot(scaled, wg[pl.ds(offset, 256), :])
        kv_acc = kv_acc + dot(scaled, wkv[pl.ds(offset, 256), :])
    wait_recv(hf, 1)
    rest = []
    for i in range(4):
        square, scaled, offset = features(oh, i)
        squares = squares + square
        rest.append((scaled, offset))
        q_acc = q_acc + dot(scaled, wq[pl.ds(offset, 256), :])
    row_scale = lax.rsqrt(jnp.sum(squares, axis=-1, keepdims=True) / WIDTH + EPS)
    query = normed_rotated(q_acc * row_scale, qgain_ref[...]).astype(BF)
    qs[...] = query
    qb[n] = query

    for dx, dc in FAR:
        send(qs, qf.at[n], 16, 3, (r, head_at(dx, 1, dc)))
    for dx, dc in NEAR:
        send(qs, qb.at[n], 1, 2, (r, head_at(dx, 0, dc)))

    for scaled, offset in rest:
        g_acc = g_acc + dot(scaled, wg[pl.ds(offset, 256), :])
        kv_acc = kv_acc + dot(scaled, wkv[pl.ds(offset, 256), :])
    gate = jax.nn.sigmoid(g_acc * row_scale)
    projected = kv_acc * row_scale
    fresh = jnp.where(c == 0, normed_rotated(projected, kgain_ref[...]), projected).astype(BF)
    fs[...] = fresh
    fb[c] = fresh
    send(fs, fb.at[c], 2, 4, (r, head_at(0, 0, 1)))

    def attend(half, queries, sums):
        q = queries[...].astype(F32).reshape(64, 128).astype(BF)

        def weights(keys, live):
            scores = dot_nt(q, keys) * SCALE
            rows = lax.broadcasted_iota(jnp.int32, scores.shape, 0)
            cols = lax.broadcasted_iota(jnp.int32, scores.shape, 1)
            seen = ((cols & 7) == (rows >> 4) * 2 + half) & live(rows, cols)
            return jnp.where(seen, jnp.exp(scores), 0.0)

        def tail_live(rows, cols):
            limit = jnp.where(cols < 256, jnp.where(cols < 128, tails[0], tails[1]),
                              jnp.where(cols < 384, tails[2], tails[3])) - h * 16
            return ((cols >> 7) == ((rows & 7) >> 1)) & (((cols >> 3) & 15) < limit)

        w_prefix = weights(kc[pl.ds(0, 2048), :], lambda rows, cols: (cols >> 3) < plen - h * 256)
        w_tail = weights(kc[pl.ds(2048, 512), :], tail_live)
        numer = dot(w_prefix.astype(BF), vc[pl.ds(0, 2048), :]) + dot(w_tail.astype(BF), vc[pl.ds(2048, 512), :])
        total = jnp.sum(w_prefix, axis=-1, keepdims=True) + jnp.sum(w_tail, axis=-1, keepdims=True)
        high = total.astype(BF).astype(F32)
        lanes = lax.broadcasted_iota(jnp.int32, (64, 128), 1)
        totals = jnp.where(lanes < 64, high, total - high)
        both = jnp.concatenate([numer.reshape(8, 8, 128), totals.reshape(8, 8, 128)], axis=1)
        sums[...] = both.astype(BF)

    wait_recv(qb.at[pl.ds(0, 7)], 2)
    attend(zh, qb, mb)
    nb[n] = mb[n]
    for dx, dc in NEAR:
        send(mb.at[near_at(dx, dc)], nb.at[n], 3, 5, (r, head_at(dx, 0, dc)))
    wait_recv(qf, 3)
    attend(oh, qf, mf)
    for dx, dc in FAR:
        send(mf.at[near_at(dx, dc)], nf.at[n], 17, 6, (r, head_at(dx, 1, dc)))

    wait_recv(fb.at[0], 4)
    scores = dot_nt(query, fb[0]) * SCALE
    rows = lax.broadcasted_iota(jnp.int32, (8, 8), 0)
    cols = lax.broadcasted_iota(jnp.int32, (8, 8), 1)
    w_fresh = jnp.where((rows // 2 == cols // 2) & (cols <= rows), jnp.exp(scores), 0.0)
    numer = dot(w_fresh.astype(BF), fb[1])
    total = jnp.sum(w_fresh, axis=-1, keepdims=True)

    wait_recv(nb.at[pl.ds(0, 7)], 5)
    sums = jnp.sum(nb[...].astype(F32), axis=0)
    wait_recv(nf, 6)
    sums = sums + jnp.sum(nf[...].astype(F32), axis=0)
    numer = numer + sums[:8]
    total = total + sums[8:, 0:1] + sums[8:, 64:65]
    gated = (numer / total * gate).astype(BF)

    mixed = dot(gated, wo[...])
    for place in range(8):
        px, pc = place // 2, place % 2
        for j, block in enumerate((8 * pc + px, 8 * pc + 4 + px, 4 * px + pc, 4 * px + 2 + pc)):
            sb[place, j] = mixed[:, block * 128:(block + 1) * 128].astype(BF)
    rb[n] = sb[n]
    for dx, dc in NEAR:
        send(sb.at[near_at(dx, dc)], rb.at[n], 4, 7, (r, head_at(dx, 0, dc)))
    wait_recv(rb.at[pl.ds(0, 7)], 7)
    sums = jnp.sum(rb[...].astype(F32), axis=0)
    first = jnp.where(zh == 0, 1.0, 0.0)

    def hidden_at(place):
        both = jnp.where(x // 2 == 0, hb[place].astype(F32), hf[place].astype(F32))
        return both * first

    tb[0] = (sums[0] + hidden_at(4 * c + x % 2)).astype(BF)
    tb[1] = (sums[1] + hidden_at(4 * c + 2 + x % 2)).astype(BF)
    residual = [sums[2] + hb[n].astype(F32) * first, sums[3] + hf[n].astype(F32) * first]

    slot = (zh * 4 + zz) * 2 + c
    target = y * 8 + 2 * x + zb
    for dz in (1, 0):
        for dx, dc in FAR:
            if dz or dx or dc:
                send(tb, xb.at[slot], 5, 8, (target, head_at(dx, dz, dc)))

    @pl.when(x != zz)
    def _():
        send(tb, xb.at[slot], 14, 8, (target, h))

        wait_recv(xb, 8)

    @pl.when(x == zz)
    def _():
        xb[slot] = tb[...]
        wait_recv(xb.at[pl.ds(0, 15)], 8)

    halves = xb[...].astype(F32)
    attended = halves[:8] + halves[8:]
    squares = jnp.zeros((32, 128), F32)
    parts = []
    for fy in range(4):
        block = jnp.concatenate([attended[i * 2 + fy // 2, fy % 2] for i in range(4)], axis=0)
        squares = squares + block * block
        offset = pl.multiple_of((fy * 4 + zz) * 128, 128)
        parts.append((block * mgain_ref[:, pl.ds(offset, 128)]).astype(BF))
    mlp_in = jnp.concatenate(parts, axis=1)
    square = jnp.sum(squares, axis=-1, keepdims=True)
    high = square.astype(BF).astype(F32)
    lanes = lax.broadcasted_iota(jnp.int32, (32, 128), 1)
    square = jnp.where(lanes < 64, high, square - high)
    wait_recv(wgate.at[pl.ds(0, 7)], 21)
    wait_recv(wup.at[pl.ds(0, 7)], 22)
    gate_part = dot(mlp_in, wgate[...].reshape(512, 384))
    up_part = dot(mlp_in, wup[...].reshape(512, 384))

    for i in range(4):
        rows = slice(i * 8, i * 8 + 8)
        ps[i, :, 0:384] = gate_part[rows].astype(BF)
        ps[i, :, 384:768] = up_part[rows].astype(BF)
        ps[i, :, 768:896] = square[rows].astype(BF)
    pb[zz] = ps[zz]
    for dzz in (2, 1, 3):
        to = (zz + dzz) % 4
        send(ps.at[to], pb.at[zz], 6, 9, (y * 8 + 2 * to + zb, h))
    wait_recv(pb.at[pl.ds(0, 3)], 9)
    sums = jnp.sum(pb[...].astype(F32), axis=0)
    scale = lax.rsqrt((sums[:, 768:769] + sums[:, 832:833]) / WIDTH + EPS)
    act = (jax.nn.silu(sums[:, 0:384] * scale) * (sums[:, 384:768] * scale)).astype(BF)

    down = dot(act, wdown[...])
    for place in range(8):
        px, pc = place // 2, place % 2
        for j, block in enumerate((4 * px + pc, 4 * px + 2 + pc)):
            ds_[place, j] = down[:, block * 128:(block + 1) * 128].astype(BF)
    db[n] = ds_[n]
    for dx, dc in NEAR:
        send(ds_.at[near_at(dx, dc)], db.at[n], 7, 10, (r, head_at(dx, 0, dc)))
    wait_recv(db.at[pl.ds(0, 7)], 10)
    sums = jnp.sum(db[...].astype(F32), axis=0)
    for j in range(2):
        value = (sums[j] + residual[j]).astype(BF)
        ys[j] = value
        yb[y, j] = value

    for dy in (2, 1, 3):
        send(ys, yb.at[y], 8, 11, (((y + dy) % 4) * 8 + z, h))
    wait_recv(yb.at[pl.ds(0, 3)], 11)
    for i in range(8):
        zs[i] = yb[owners[i] // 8]
    zb_[zh * 8 + z] = zs[z]
    for dz, dzl in [(1, 0)] + [(d, e) for e in (4, 3, 5, 2, 6, 1, 7) for d in (1, 0)]:
        to = (z + dzl) % 8
        send(zs.at[to], zb_.at[zh * 8 + z], 9, 12, (y * 8 + to, head_at(0, dz, 0)))
    wait_recv(zb_.at[pl.ds(0, 15)], 12)
    wait_recv(gb.at[0], 20)
    from_z = owners[8] % 8
    final = (zb_[from_z].astype(F32) + zb_[8 + from_z].astype(F32)).astype(BF).astype(F32)
    out_ref[...] = jnp.where(zh == 0, final[0], final[1]).astype(BF)

    square = jnp.sum(final[0] * final[0] + final[1] * final[1], axis=-1, keepdims=True)
    product = jnp.sum(final[0] * gb[0] + final[1] * gb[1], axis=-1, keepdims=True)
    both = jnp.where(lane < 64, square, product)
    cs[...] = both
    cb[n] = both
    for dx, dc in NEAR:
        send(cs, cb.at[n], 10, 13, (r, head_at(dx, 0, dc)))
    wait_recv(cb.at[pl.ds(0, 7)], 13)
    sums = jnp.sum(cb[...], axis=0)
    score_ref[...] = jnp.broadcast_to(sums[:, 64:65] * lax.rsqrt(sums[:, 0:1] / WIDTH + EPS), (8, 128))

    wait_send(hb.at[pl.ds(0, 7)], 0)
    wait_send(hf, 15)
    wait_send(qb.at[pl.ds(0, 7)], 1)
    wait_send(qf, 16)
    wait_send(fb.at[0], 2)
    wait_send(nb.at[pl.ds(0, 7)], 3)
    wait_send(nf, 17)
    wait_send(rb.at[pl.ds(0, 7)], 4)
    wait_send(xb.at[pl.ds(0, 15)], 5)

    @pl.when(x != zz)
    def _():
        wait_send(xb.at[0], 14)
    wait_send(pb.at[pl.ds(0, 3)], 6)
    wait_send(db.at[pl.ds(0, 7)], 7)
    wait_send(yb.at[pl.ds(0, 3)], 8)
    wait_send(zb_.at[pl.ds(0, 15)], 9)
    wait_send(cb.at[pl.ds(0, 7)], 10)
    wait_send(gb.at[0], 11)
    wait_send(wgate.at[pl.ds(0, 7)], 12)
    wait_send(wup.at[pl.ds(0, 7)], 13)


def shards(
    hidden, attn_gain, q_weight, gate_weight, key_value_weight, q_gain, k_gain, out_weight,
    prompt_key_cache, prompt_value_cache, tail_key_cache, tail_value_cache, mlp_gain, mlp_gate,
    mlp_up, mlp_down, final_gain, score_weight, prompt_lengths, tail_lengths, group_prompt,
):
    vmem = pl.BlockSpec(memory_space=pltpu.VMEM)
    smem = pl.BlockSpec(memory_space=pltpu.SMEM)
    hbm = pl.BlockSpec(memory_space=pl.ANY)

    def blocks(*shape, kind=BF):
        return pltpu.VMEM(shape, kind)

    out, score = pl.pallas_call(
        kernel,
        out_shape=(jax.ShapeDtypeStruct((8, 128), BF), jax.ShapeDtypeStruct((8, 128), F32)),
        in_specs=[smem] * 3 + [vmem] * 7 + [hbm] * 11,
        out_specs=(vmem, vmem),
        scratch_shapes=[
            blocks(2048, 128), blocks(2048, 128), blocks(2048, 128), blocks(128, 2048),
            blocks(2560, 128), blocks(2560, 128),
            blocks(8, 64, 384), blocks(8, 64, 384), blocks(384, 2048),
            blocks(8, 8, 128), blocks(8, 8, 128),
            blocks(8, 128), blocks(8, 8, 128), blocks(8, 8, 128),
            blocks(8, 128), blocks(2, 8, 128),
            blocks(8, 16, 128), blocks(8, 16, 128),
            blocks(8, 16, 128), blocks(8, 16, 128),
            blocks(8, 4, 8, 128), blocks(8, 4, 8, 128),
            blocks(2, 8, 128), blocks(16, 2, 8, 128),
            blocks(4, 8, 896), blocks(4, 8, 896),
            blocks(8, 2, 8, 128), blocks(8, 2, 8, 128),
            blocks(2, 8, 128), blocks(4, 2, 8, 128),
            blocks(8, 2, 8, 128), blocks(16, 2, 8, 128),
            blocks(8, 128, kind=F32), blocks(8, 8, 128, kind=F32),
            blocks(8, 128, kind=F32), blocks(2, 8, 128, kind=F32),
            pltpu.SemaphoreType.DMA((11,)),
            pltpu.SemaphoreType.DMA((18,)),
            pltpu.SemaphoreType.DMA((23,)),
        ],
        compiler_params=pltpu.CompilerParams(
            collective_id=0, has_side_effects=True, vmem_limit_bytes=60 << 20
        ),
    )(
        prompt_lengths, tail_lengths, group_prompt,
        hidden, attn_gain.reshape(1, -1), q_gain.reshape(1, -1), k_gain.reshape(1, -1),
        mlp_gain.reshape(1, -1), final_gain.reshape(1, -1), score_weight.reshape(1, -1),
        q_weight, gate_weight, key_value_weight, out_weight,
        prompt_key_cache.reshape(-1, 128), prompt_value_cache.reshape(-1, 128),
        tail_key_cache.reshape(-1, 128), tail_value_cache.reshape(-1, 128),
        mlp_gate, mlp_up, mlp_down,
    )
    return out, score[:, 0]


def solution(mesh):
    return jax.shard_map(
        shards,
        mesh=mesh,
        in_specs=(
            P("req", "head"),
            P(),
            P(None, "head"),
            P(None, "head"),
            P(None, "head"),
            P(),
            P(),
            P("head", None),
            P("req", "head", None, None),
            P("req", "head", None, None),
            P("req", None, "head", None, None),
            P("req", None, "head", None, None),
            P(),
            P("req", "head"),
            P("req", "head"),
            P("head", None),
            P("head"),
            P("head"),
            P(),
            P(),
            P(),
        ),
        out_specs=(P("req", "head"), P("req")),
        check_vma=False,
    )
```

```python
import functools
import math

import jax
import jax.numpy as jnp
from jax import lax
from jax.experimental import pallas as pl
from jax.experimental.pallas import tpu as pltpu
from jax.sharding import PartitionSpec as P

EPS = 1e-06
THETA = 1000000.0
MESH = pl.DeviceIdType.MESH
BF = jnp.bfloat16
F32 = jnp.float32
WIDTH = 2048
SCALE = 1.0 / math.sqrt(128.0)

NEAR = [(2, 1), (2, 0), (1, 1), (3, 1), (1, 0), (3, 0), (0, 1)]
FAR = [(2, 1), (2, 0), (1, 1), (3, 1), (1, 0), (3, 0), (0, 1), (0, 0)]

SPREAD = sorted(
    ((dy, dx, dc) for dy in range(4) for dx in range(4) for dc in range(2) if dy or dx or dc),
    key=lambda at: -(min(at[0], 4 - at[0]) + min(at[1], 4 - at[1]) + at[2] * 0.5),
)


def dot(a, b):
    return jnp.dot(a, b, preferred_element_type=F32)


def dot_nt(a, b):
    return lax.dot_general(a, b, (((1,), (1,)), ((), ())), preferred_element_type=F32)


def kernel(
    plen_hbm, tlen_hbm, gp_hbm, hidden_hbm, again_hbm, qgain_hbm, kgain_hbm, mgain_hbm, fgain_hbm, sw_hbm,
    wq_hbm, wg_hbm, wkv_hbm, wo_hbm, pk_hbm, pv_hbm, tk_hbm, tv_hbm, mg_hbm, mu_hbm, md_hbm,
    out_ref, score_ref,
    plen_ref, tlen_ref, gp_ref, again_ref, qgain_ref, kgain_ref, mgain_ref, fgain_ref, sw_ref,
    wq, wg, wkv, wo, kc, vc, wmlp, wdown,
    hb, hf, qs, qb, qf, fs, fb, mb, mf, nb, nf, sb, rb, tb, xb, ps, pb, ds_, db, yb, zs, zb_, cs, cb, gs, gb,
    lsem, ssem, rsem,
):
    r = lax.axis_index("req")
    h = lax.axis_index("head")
    y, z = lax.div(r, 8), lax.rem(r, 8)
    x, zh, c = lax.div(h, 4), lax.rem(lax.div(h, 2), 2), lax.rem(h, 2)
    zz, zb = lax.div(z, 2), lax.rem(z, 2)
    n = x * 2 + c
    oh = 1 - zh

    def around(value, size):
        shifted = [value] + [value + i for i in range(1, size)]
        return [jnp.where(v >= size, v - size, v) for v in shifted]

    xs, ys_, zzs, zls = around(x, 4), around(y, 4), around(zz, 4), around(z, 8)
    zhs, cc, zbs = around(zh, 2), around(c, 2), around(zb, 2)

    def head_at(dx, dz, dc):
        return xs[dx] * 4 + zhs[dz] * 2 + cc[dc]

    def near_at(dx, dc):
        return xs[dx] * 2 + cc[dc]

    def send(src, dst, phase, at, dev):
        pltpu.make_async_remote_copy(
            src_ref=src, dst_ref=dst, send_sem=ssem.at[phase], recv_sem=rsem.at[at],
            device_id=dev, device_id_type=MESH,
        ).start()

    def waiter(ref, phase, at):
        return pltpu.make_async_remote_copy(
            src_ref=ref, dst_ref=ref, send_sem=ssem.at[phase], recv_sem=rsem.at[at],
            device_id=(r, head_at(0, 0, 1)), device_id_type=MESH,
        )

    def wait_recv(ref, at):
        waiter(ref, 0, at).wait_recv()

    def wait_send(ref, phase):
        waiter(ref, phase, 0).wait_send()

    own_w = y * 2 + zb
    hidden_copy = pltpu.make_async_copy(hidden_hbm, hb.at[n], lsem.at[0])
    hidden_copy.start()
    bar = pltpu.get_barrier_semaphore()

    def greet(dev):
        pl.semaphore_signal(bar, inc=1, device_id=dev, device_id_type=MESH)

    for dx, dc in FAR:
        greet((r, head_at(dx, 1, dc)))
    for dzz in (2, 1, 3, 0):
        for dz in (1, 0):
            for dc in (1, 0):
                dev = (y * 8 + zzs[dzz] * 2 + zb, zz * 4 + zhs[dz] * 2 + cc[dc])
                if dzz == 0 and dz == 0 and dc == 0:
                    @pl.when(x != zz)
                    def _():
                        greet(dev)
                else:
                    greet(dev)
    for dzl in (4, 3, 5, 2, 6, 1, 7):
        for dz in (1, 0):
            greet((y * 8 + zls[dzl], head_at(0, dz, 0)))
    for dx, dc in NEAR:
        greet((r, head_at(dx, 0, dc)))
    for dy in (2, 1, 3):
        for dzb in (1, 0):
            greet((ys_[dy] * 8 + zz * 2 + zbs[dzb], h))

    local = [
        (mg_hbm, wmlp.at[own_w, :, pl.ds(0, 384)]), (mu_hbm, wmlp.at[own_w, :, pl.ds(384, 384)]),
        (fgain_hbm, fgain_ref), (sw_hbm, sw_ref), (plen_hbm, plen_ref), (tlen_hbm, tlen_ref), (gp_hbm, gp_ref),
        (again_hbm, again_ref), (wq_hbm, wq), (qgain_hbm, qgain_ref), (kgain_hbm, kgain_ref),
        (wg_hbm, wg), (wkv_hbm, wkv),
        (pk_hbm, kc.at[pl.ds(0, 2048)]), (tk_hbm, kc.at[pl.ds(2048, 512)]),
        (pv_hbm, vc.at[pl.ds(0, 2048)]), (tv_hbm, vc.at[pl.ds(2048, 512)]),
        (wo_hbm, wo), (mgain_hbm, mgain_ref), (md_hbm, wdown),
    ]
    copies = [pltpu.make_async_copy(s, d, lsem.at[i + 1]) for i, (s, d) in enumerate(local)]
    for cp in copies:
        cp.start()
    hidden_copy.wait()
    pl.semaphore_wait(bar, 50 + jnp.where(x != zz, 1, 0))

    for dx, dc in FAR:
        send(hb.at[n], hf.at[n], 15, 1, (r, head_at(dx, 1, dc)))
    for dx, dc in NEAR:
        send(hb.at[n], hb.at[n], 0, 0, (r, head_at(dx, 0, dc)))

    copies[0].wait()
    copies[1].wait()
    for dy in (2, 1, 3, 0):
        for dzb in (1, 0):
            if dy or dzb:
                send(wmlp.at[own_w], wmlp.at[own_w], 12, 21, (ys_[dy] * 8 + zz * 2 + zbs[dzb], h))
    for i in range(2, 20):
        copies[i].wait()
    gs[...] = jnp.broadcast_to(fgain_ref[...] * sw_ref[...], (8, 128))
    gb[zh] = gs[...]
    send(gs, gb.at[zh], 11, 20, (r, head_at(0, 1, 0)))

    prompt = gp_ref[r]
    plen = plen_ref[prompt]
    tails = [tlen_ref[i, prompt] for i in range(4)]

    def find(g, found):
        value = gp_ref[g]
        mine = jnp.where(value == r, g, found[8])
        return tuple(jnp.where(value == y * 8 + i, g, found[i]) for i in range(8)) + (mine,)

    owners = lax.fori_loop(0, 32, find, (jnp.int32(0),) * 9)

    row = lax.broadcasted_iota(jnp.int32, (8, 128), 0)
    lane = lax.broadcasted_iota(jnp.int32, (8, 128), 1)
    position = plen + row % 2
    for i in range(4):
        position = position + jnp.where(row // 2 == i, tails[i], 0)
    half_lane = (lane % 64).astype(F32)
    frequency = jnp.exp(-math.log(THETA) * 2.0 * half_lane / 128.0)
    angle = position.astype(F32) * frequency
    cosine = jnp.cos(angle)
    sine = jnp.sin(angle)
    sine = jnp.where(lane < 64, -sine, sine)

    def normed_rotated(value, gain):
        value = value * lax.rsqrt(jnp.mean(value * value, axis=-1, keepdims=True) + EPS) * gain
        return value * cosine + pltpu.roll(value, 64, 1) * sine

    def features(half, at):
        place = at * 4 + half * 2
        offset = pl.multiple_of(place * 128, 256)
        ref = hb if half is zh else hf
        value = jnp.concatenate([ref[at * 2].astype(F32), ref[at * 2 + 1].astype(F32)], axis=1)
        scaled = (value * again_ref[:, pl.ds(offset, 256)]).astype(BF)
        return value * value, scaled, offset

    wait_recv(hb.at[pl.ds(0, 7)], 0)
    squares = jnp.zeros((8, 256), F32)
    q_acc = jnp.zeros((8, 128), F32)
    g_acc = jnp.zeros((8, 128), F32)
    kv_acc = jnp.zeros((8, 128), F32)
    for i in range(4):
        square, scaled, offset = features(zh, i)
        squares = squares + square
        q_acc = q_acc + dot(scaled, wq[pl.ds(offset, 256), :])
        g_acc = g_acc + dot(scaled, wg[pl.ds(offset, 256), :])
        kv_acc = kv_acc + dot(scaled, wkv[pl.ds(offset, 256), :])
    wait_recv(hf, 1)
    rest = []
    for i in range(4):
        square, scaled, offset = features(oh, i)
        squares = squares + square
        rest.append((scaled, offset))
        q_acc = q_acc + dot(scaled, wq[pl.ds(offset, 256), :])
    row_scale = lax.rsqrt(jnp.sum(squares, axis=-1, keepdims=True) / WIDTH + EPS)
    query = normed_rotated(q_acc * row_scale, qgain_ref[...]).astype(BF)
    qs[...] = query
    qb[n] = query

    for dx, dc in FAR:
        send(qs, qf.at[n], 16, 3, (r, head_at(dx, 1, dc)))
    for dx, dc in NEAR:
        send(qs, qb.at[n], 1, 2, (r, head_at(dx, 0, dc)))

    for scaled, offset in rest:
        g_acc = g_acc + dot(scaled, wg[pl.ds(offset, 256), :])
        kv_acc = kv_acc + dot(scaled, wkv[pl.ds(offset, 256), :])
    gate = jax.nn.sigmoid(g_acc * row_scale)
    projected = kv_acc * row_scale
    fresh = jnp.where(c == 0, normed_rotated(projected, kgain_ref[...]), projected).astype(BF)
    fs[...] = fresh
    fb[c] = fresh
    send(fs, fb.at[c], 2, 4, (r, head_at(0, 0, 1)))

    def attend(half, queries, sums):
        q = queries[...].astype(F32).reshape(64, 128).astype(BF)

        def weights(keys, live):
            scores = dot_nt(q, keys) * SCALE
            rows = lax.broadcasted_iota(jnp.int32, scores.shape, 0)
            cols = lax.broadcasted_iota(jnp.int32, scores.shape, 1)
            seen = ((cols & 7) == (rows >> 4) * 2 + half) & live(rows, cols)
            return jnp.where(seen, jnp.exp(scores), 0.0)

        def tail_live(rows, cols):
            limit = jnp.where(cols < 256, jnp.where(cols < 128, tails[0], tails[1]),
                              jnp.where(cols < 384, tails[2], tails[3])) - h * 16
            return ((cols >> 7) == ((rows & 7) >> 1)) & (((cols >> 3) & 15) < limit)

        w_prefix = weights(kc[pl.ds(0, 2048), :], lambda rows, cols: (cols >> 3) < plen - h * 256)
        w_tail = weights(kc[pl.ds(2048, 512), :], tail_live)
        numer = dot(w_prefix.astype(BF), vc[pl.ds(0, 2048), :]) + dot(w_tail.astype(BF), vc[pl.ds(2048, 512), :])
        total = jnp.sum(w_prefix, axis=-1, keepdims=True) + jnp.sum(w_tail, axis=-1, keepdims=True)
        high = total.astype(BF).astype(F32)
        lanes = lax.broadcasted_iota(jnp.int32, (64, 128), 1)
        totals = jnp.where(lanes < 64, high, total - high)
        both = jnp.concatenate([numer.reshape(8, 8, 128), totals.reshape(8, 8, 128)], axis=1)
        sums[...] = both.astype(BF)

    wait_recv(qb.at[pl.ds(0, 7)], 2)
    attend(zh, qb, mb)
    nb[n] = mb[n]
    for dx, dc in NEAR:
        send(mb.at[near_at(dx, dc)], nb.at[n], 3, 5, (r, head_at(dx, 0, dc)))
    wait_recv(qf, 3)
    attend(oh, qf, mf)
    for dx, dc in FAR:
        send(mf.at[near_at(dx, dc)], nf.at[n], 17, 6, (r, head_at(dx, 1, dc)))

    wait_recv(fb.at[0], 4)
    scores = dot_nt(query, fb[0]) * SCALE
    rows = lax.broadcasted_iota(jnp.int32, (8, 8), 0)
    cols = lax.broadcasted_iota(jnp.int32, (8, 8), 1)
    w_fresh = jnp.where((rows // 2 == cols // 2) & (cols <= rows), jnp.exp(scores), 0.0)
    numer = dot(w_fresh.astype(BF), fb[1])
    total = jnp.sum(w_fresh, axis=-1, keepdims=True)

    wait_recv(nb.at[pl.ds(0, 7)], 5)
    sums = jnp.sum(nb[...].astype(F32), axis=0)
    wait_recv(nf, 6)
    sums = sums + jnp.sum(nf[...].astype(F32), axis=0)
    numer = numer + sums[:8]
    total = total + sums[8:, 0:1] + sums[8:, 64:65]
    gated = (numer / total * gate).astype(BF)

    mixed = dot(gated, wo[...])
    for place in range(8):
        px, pc = place // 2, place % 2
        for j, block in enumerate((8 * pc + px, 8 * pc + 4 + px, 4 * px + pc, 4 * px + 2 + pc)):
            sb[place, j] = mixed[:, block * 128:(block + 1) * 128].astype(BF)
    rb[n] = sb[n]
    for dx, dc in NEAR:
        send(sb.at[near_at(dx, dc)], rb.at[n], 4, 7, (r, head_at(dx, 0, dc)))
    wait_recv(rb.at[pl.ds(0, 7)], 7)
    sums = jnp.sum(rb[...].astype(F32), axis=0)
    first = jnp.where(zh == 0, 1.0, 0.0)

    def hidden_at(place):
        both = jnp.where(x < 2, hb[place].astype(F32), hf[place].astype(F32))
        return both * first

    tb[0] = (sums[0] + hidden_at(4 * c + lax.rem(x, 2))).astype(BF)
    tb[1] = (sums[1] + hidden_at(4 * c + 2 + lax.rem(x, 2))).astype(BF)
    residual = [sums[2] + hb[n].astype(F32) * first, sums[3] + hf[n].astype(F32) * first]

    slot = (zh * 4 + zz) * 2 + c
    target = y * 8 + 2 * x + zb
    for dz in (1, 0):
        for dx, dc in FAR:
            if dz or dx or dc:
                send(tb, xb.at[slot], 5, 8, (target, head_at(dx, dz, dc)))

    @pl.when(x != zz)
    def _():
        send(tb, xb.at[slot], 14, 8, (target, h))

        wait_recv(xb, 8)

    @pl.when(x == zz)
    def _():
        xb[slot] = tb[...]
        wait_recv(xb.at[pl.ds(0, 15)], 8)

    halves = xb[...].astype(F32)
    attended = halves[:8] + halves[8:]
    squares = jnp.zeros((32, 128), F32)
    parts = []
    for fy in range(4):
        block = jnp.concatenate([attended[i * 2 + fy // 2, fy % 2] for i in range(4)], axis=0)
        squares = squares + block * block
        offset = pl.multiple_of((fy * 4 + zz) * 128, 128)
        parts.append((block * mgain_ref[:, pl.ds(offset, 128)]).astype(BF))
    mlp_in = jnp.concatenate(parts, axis=1)
    square = jnp.sum(squares, axis=-1, keepdims=True)
    high = square.astype(BF).astype(F32)
    lanes = lax.broadcasted_iota(jnp.int32, (32, 128), 1)
    square = jnp.where(lanes < 64, high, square - high)
    wait_recv(wmlp.at[pl.ds(0, 7)], 21)
    both = dot(mlp_in, wmlp[...].reshape(512, 768))

    for i in range(4):
        rows = slice(i * 8, i * 8 + 8)
        ps[i, :, 0:768] = both[rows].astype(BF)
        ps[i, :, 768:896] = square[rows].astype(BF)
    pb[zz] = ps[zz]
    for dzz in (2, 1, 3):
        to = zzs[dzz]
        send(ps.at[to], pb.at[zz], 6, 9, (y * 8 + 2 * to + zb, h))
    wait_recv(pb.at[pl.ds(0, 3)], 9)
    sums = jnp.sum(pb[...].astype(F32), axis=0)
    scale = lax.rsqrt((sums[:, 768:769] + sums[:, 832:833]) / WIDTH + EPS)
    act = (jax.nn.silu(sums[:, 0:384] * scale) * (sums[:, 384:768] * scale)).astype(BF)

    down = dot(act, wdown[...])
    for place in range(8):
        px, pc = place // 2, place % 2
        for j, block in enumerate((4 * px + pc, 4 * px + 2 + pc)):
            ds_[place, j] = down[:, block * 128:(block + 1) * 128].astype(BF)
    for j in range(2):
        ds_[n, j] = (ds_[n, j].astype(F32) + residual[j]).astype(BF)
    db[y * 8 + n] = ds_[n]
    for dy, dx, dc in SPREAD:
        send(ds_.at[near_at(dx, dc)], db.at[y * 8 + n], 7, 10, (ys_[dy] * 8 + z, head_at(dx, 0, dc)))
    wait_recv(db.at[pl.ds(0, 31)], 10)
    for i in range(4):
        yb[i] = jnp.sum(db[pl.ds(i * 8, 8)].astype(F32), axis=0).astype(BF)

    for i in range(8):
        zs[i] = yb[lax.div(owners[i], 8)]
    zb_[zh * 8 + z] = zs[z]
    for dz, dzl in [(1, 0)] + [(d, e) for e in (4, 3, 5, 2, 6, 1, 7) for d in (1, 0)]:
        to = zls[dzl]
        send(zs.at[to], zb_.at[zh * 8 + z], 9, 12, (y * 8 + to, head_at(0, dz, 0)))
    wait_recv(zb_.at[pl.ds(0, 15)], 12)
    wait_recv(gb.at[0], 20)
    from_z = lax.rem(owners[8], 8)
    final = (zb_[from_z].astype(F32) + zb_[8 + from_z].astype(F32)).astype(BF).astype(F32)
    out_ref[...] = jnp.where(zh == 0, final[0], final[1]).astype(BF)

    square = jnp.sum(final[0] * final[0] + final[1] * final[1], axis=-1, keepdims=True)
    product = jnp.sum(final[0] * gb[0] + final[1] * gb[1], axis=-1, keepdims=True)
    both = jnp.where(lane < 64, square, product)
    cs[...] = both
    cb[n] = both
    for dx, dc in NEAR:
        send(cs, cb.at[n], 10, 13, (r, head_at(dx, 0, dc)))
    wait_recv(cb.at[pl.ds(0, 7)], 13)
    sums = jnp.sum(cb[...], axis=0)
    score_ref[...] = jnp.broadcast_to(sums[:, 64:65] * lax.rsqrt(sums[:, 0:1] / WIDTH + EPS), (8, 128))

    wait_send(hb.at[pl.ds(0, 7)], 0)
    wait_send(hf, 15)
    wait_send(qb.at[pl.ds(0, 7)], 1)
    wait_send(qf, 16)
    wait_send(fb.at[0], 2)
    wait_send(nb.at[pl.ds(0, 7)], 3)
    wait_send(nf, 17)
    wait_send(rb.at[pl.ds(0, 7)], 4)
    wait_send(xb.at[pl.ds(0, 15)], 5)

    @pl.when(x != zz)
    def _():
        wait_send(xb.at[0], 14)
    wait_send(pb.at[pl.ds(0, 3)], 6)
    wait_send(db.at[pl.ds(0, 31)], 7)
    wait_send(zb_.at[pl.ds(0, 15)], 9)
    wait_send(cb.at[pl.ds(0, 7)], 10)
    wait_send(gb.at[0], 11)
    wait_send(wmlp.at[pl.ds(0, 7)], 12)


def shards(
    hidden, attn_gain, q_weight, gate_weight, key_value_weight, q_gain, k_gain, out_weight,
    prompt_key_cache, prompt_value_cache, tail_key_cache, tail_value_cache, mlp_gain, mlp_gate,
    mlp_up, mlp_down, final_gain, score_weight, prompt_lengths, tail_lengths, group_prompt,
):
    vmem = pl.BlockSpec(memory_space=pltpu.VMEM)
    hbm = pl.BlockSpec(memory_space=pl.ANY)

    def blocks(*shape, kind=BF):
        return pltpu.VMEM(shape, kind)

    out, score = pl.pallas_call(
        kernel,
        out_shape=(jax.ShapeDtypeStruct((8, 128), BF), jax.ShapeDtypeStruct((8, 128), F32)),
        in_specs=[hbm] * 21,
        out_specs=(vmem, vmem),
        scratch_shapes=[
            pltpu.SMEM((32,), jnp.int32), pltpu.SMEM((4, 32), jnp.int32), pltpu.SMEM((32,), jnp.int32),
            blocks(1, 2048, kind=F32), blocks(1, 128, kind=F32), blocks(1, 128, kind=F32),
            blocks(1, 2048, kind=F32), blocks(1, 128, kind=F32), blocks(1, 128, kind=F32),
            blocks(2048, 128), blocks(2048, 128), blocks(2048, 128), blocks(128, 2048),
            blocks(2560, 128), blocks(2560, 128),
            blocks(8, 64, 768), blocks(384, 2048),
            blocks(8, 8, 128), blocks(8, 8, 128),
            blocks(8, 128), blocks(8, 8, 128), blocks(8, 8, 128),
            blocks(8, 128), blocks(2, 8, 128),
            blocks(8, 16, 128), blocks(8, 16, 128),
            blocks(8, 16, 128), blocks(8, 16, 128),
            blocks(8, 4, 8, 128), blocks(8, 4, 8, 128),
            blocks(2, 8, 128), blocks(16, 2, 8, 128),
            blocks(4, 8, 896), blocks(4, 8, 896),
            blocks(8, 2, 8, 128), blocks(32, 2, 8, 128),
            blocks(4, 2, 8, 128),
            blocks(8, 2, 8, 128), blocks(16, 2, 8, 128),
            blocks(8, 128, kind=F32), blocks(8, 8, 128, kind=F32),
            blocks(8, 128, kind=F32), blocks(2, 8, 128, kind=F32),
            pltpu.SemaphoreType.DMA((21,)),
            pltpu.SemaphoreType.DMA((18,)),
            pltpu.SemaphoreType.DMA((23,)),
        ],
        compiler_params=pltpu.CompilerParams(
            collective_id=0, has_side_effects=True, vmem_limit_bytes=60 << 20
        ),
    )(
        prompt_lengths, tail_lengths.T, group_prompt,
        hidden, attn_gain.reshape(1, -1), q_gain.reshape(1, -1), k_gain.reshape(1, -1),
        mlp_gain.reshape(1, -1), final_gain.reshape(1, -1), score_weight.reshape(1, -1),
        q_weight, gate_weight, key_value_weight, out_weight,
        prompt_key_cache.reshape(-1, 128), prompt_value_cache.reshape(-1, 128),
        tail_key_cache.reshape(-1, 128), tail_value_cache.reshape(-1, 128),
        mlp_gate, mlp_up, mlp_down,
    )
    return out, score[:, 0]


def solution(mesh):
    return jax.shard_map(
        shards,
        mesh=mesh,
        in_specs=(
            P("req", "head"),
            P(),
            P(None, "head"),
            P(None, "head"),
            P(None, "head"),
            P(),
            P(),
            P("head", None),
            P("req", "head", None, None),
            P("req", "head", None, None),
            P("req", None, "head", None, None),
            P("req", None, "head", None, None),
            P(),
            P("req", "head"),
            P("req", "head"),
            P("head", None),
            P("head"),
            P("head"),
            P(),
            P(),
            P(),
        ),
        out_specs=(P("req", "head"), P("req")),
        check_vma=False,
    )
```

```python
import functools
import math

import jax
import jax.numpy as jnp
from jax import lax
from jax.experimental import pallas as pl
from jax.experimental.pallas import tpu as pltpu
from jax.sharding import PartitionSpec as P

EPS = 1e-06
THETA = 1000000.0
MESH = pl.DeviceIdType.MESH
BF = jnp.bfloat16
F32 = jnp.float32
WIDTH = 2048
SCALE = 1.0 / math.sqrt(128.0)

NEAR = [(2, 1), (2, 0), (1, 1), (3, 1), (1, 0), (3, 0), (0, 1)]
FAR = [(2, 1), (2, 0), (1, 1), (3, 1), (1, 0), (3, 0), (0, 1), (0, 0)]

SPREAD = sorted(
    ((dy, dx, dc) for dy in range(4) for dx in range(4) for dc in range(2) if dy or dx or dc),
    key=lambda at: -(min(at[0], 4 - at[0]) + min(at[1], 4 - at[1]) + at[2] * 0.5),
)


def dot(a, b):
    return jnp.dot(a, b, preferred_element_type=F32)


def dot_nt(a, b):
    return lax.dot_general(a, b, (((1,), (1,)), ((), ())), preferred_element_type=F32)


def kernel(
    plen_hbm, tlen_hbm, gp_hbm, hidden_hbm, again_hbm, qgain_hbm, kgain_hbm, mgain_hbm, fgain_hbm, sw_hbm,
    wq_hbm, wg_hbm, wkv_hbm, wo_hbm, pk_hbm, pv_hbm, tk_hbm, tv_hbm, mg_hbm, mu_hbm, md_hbm,
    out_ref, score_ref,
    plen_ref, tlen_ref, gp_ref, again_ref, qgain_ref, kgain_ref, mgain_ref, fgain_ref, sw_ref,
    wq, wg, wkv, wo, kc, vc, wmlp, wfar, wdown,
    hb, hf, qs, qb, qf, fs, fb, mb, mf, nb, nf, sb, rb, tb, xb, ps, pb, ds_, db, yb, zs, zb_, cs, cb, gs, gb,
    lsem, ssem, rsem, qsem,
):
    r = lax.axis_index("req")
    h = lax.axis_index("head")
    y, z = lax.div(r, 8), lax.rem(r, 8)
    x, zh, c = lax.div(h, 4), lax.rem(lax.div(h, 2), 2), lax.rem(h, 2)
    zt, zq = lax.div(z, 4), lax.rem(z, 4)
    n = x * 2 + c
    oh = 1 - zh

    def around(value, size):
        shifted = [value] + [value + i for i in range(1, size)]
        return [jnp.where(v >= size, v - size, v) for v in shifted]

    xs, ys_, zqs, zls = around(x, 4), around(y, 4), around(zq, 4), around(z, 8)
    zhs, cc = around(zh, 2), around(c, 2)
    own_w, other_w = y * 2 + zt, y * 2 + 1 - zt
    across = (y * 8 + (1 - zt) * 4 + zq, h)

    def head_at(dx, dz, dc):
        return xs[dx] * 4 + zhs[dz] * 2 + cc[dc]

    def near_at(dx, dc):
        return xs[dx] * 2 + cc[dc]

    def send(src, dst, phase, at, dev):
        pltpu.make_async_remote_copy(
            src_ref=src, dst_ref=dst, send_sem=ssem.at[phase], recv_sem=rsem.at[at],
            device_id=dev, device_id_type=MESH,
        ).start()

    def waiter(ref, phase, at):
        return pltpu.make_async_remote_copy(
            src_ref=ref, dst_ref=ref, send_sem=ssem.at[phase], recv_sem=rsem.at[at],
            device_id=(r, head_at(0, 0, 1)), device_id_type=MESH,
        )

    def wait_recv(ref, at):
        waiter(ref, 0, at).wait_recv()

    def wait_send(ref, phase):
        waiter(ref, phase, 0).wait_send()

    hidden_copy = pltpu.make_async_copy(hidden_hbm, hb.at[n], lsem.at[0])
    hidden_copy.start()
    bar = pltpu.get_barrier_semaphore()

    def greet(dev):
        pl.semaphore_signal(bar, inc=1, device_id=dev, device_id_type=MESH)

    for dx, dc in FAR:
        greet((r, head_at(dx, 1, dc)))
    greet(across)
    for dzq in (2, 3, 1):
        greet((y * 8 + zt * 4 + zqs[dzq], h))
    for dy in (2, 1, 3):
        greet((ys_[dy] * 8 + z, h))
    for dx, dc in NEAR:
        greet((r, head_at(dx, 0, dc)))

    local = [
        (mg_hbm, wmlp.at[own_w, :, pl.ds(0, 384)]), (mu_hbm, wmlp.at[own_w, :, pl.ds(384, 384)]),
        (fgain_hbm, fgain_ref), (sw_hbm, sw_ref), (plen_hbm, plen_ref), (tlen_hbm, tlen_ref), (gp_hbm, gp_ref),
        (again_hbm, again_ref), (wq_hbm, wq), (qgain_hbm, qgain_ref), (kgain_hbm, kgain_ref),
        (wg_hbm, wg), (wkv_hbm, wkv),
        (pk_hbm, kc.at[pl.ds(0, 2048)]), (tk_hbm, kc.at[pl.ds(2048, 512)]),
        (pv_hbm, vc.at[pl.ds(0, 2048)]), (tv_hbm, vc.at[pl.ds(2048, 512)]),
        (wo_hbm, wo), (mgain_hbm, mgain_ref), (md_hbm, wdown),
    ]
    copies = [pltpu.make_async_copy(s, d, lsem.at[i + 1]) for i, (s, d) in enumerate(local)]
    for cp in copies:
        cp.start()
    hidden_copy.wait()
    pl.semaphore_wait(bar, 22)

    for dx, dc in FAR:
        send(hb.at[n], hf.at[n], 15, 1, (r, head_at(dx, 1, dc)))
    for dx, dc in NEAR:
        send(hb.at[n], hb.at[n], 0, 0, (r, head_at(dx, 0, dc)))

    copies[0].wait()
    copies[1].wait()
    send(wmlp.at[own_w], wfar, 13, 22, across)
    for dy in (2, 1, 3):
        send(wmlp.at[own_w], wmlp.at[own_w], 12, 21, (ys_[dy] * 8 + z, h))
    for dzq in (2, 3, 1):
        pl.semaphore_signal(qsem, inc=1, device_id=(y * 8 + zt * 4 + zqs[dzq], h), device_id_type=MESH)
    for i in range(2, 20):
        copies[i].wait()
    gs[...] = jnp.broadcast_to(fgain_ref[...] * sw_ref[...], (8, 128))
    gb[zh] = gs[...]
    send(gs, gb.at[zh], 11, 20, (r, head_at(0, 1, 0)))

    prompt = gp_ref[r]
    plen = plen_ref[prompt]
    tails = [tlen_ref[i, prompt] for i in range(4)]

    def find(g, found):
        value = gp_ref[g]
        mine = jnp.where(value == r, g, found[8])
        return tuple(jnp.where(value == y * 8 + i, g, found[i]) for i in range(8)) + (mine,)

    owners = lax.fori_loop(0, 32, find, (jnp.int32(0),) * 9)

    row = lax.broadcasted_iota(jnp.int32, (8, 128), 0)
    lane = lax.broadcasted_iota(jnp.int32, (8, 128), 1)
    position = plen + row % 2
    for i in range(4):
        position = position + jnp.where(row // 2 == i, tails[i], 0)
    half_lane = (lane % 64).astype(F32)
    frequency = jnp.exp(-math.log(THETA) * 2.0 * half_lane / 128.0)
    angle = position.astype(F32) * frequency
    cosine = jnp.cos(angle)
    sine = jnp.sin(angle)
    sine = jnp.where(lane < 64, -sine, sine)

    def normed_rotated(value, gain):
        value = value * lax.rsqrt(jnp.mean(value * value, axis=-1, keepdims=True) + EPS) * gain
        return value * cosine + pltpu.roll(value, 64, 1) * sine

    def features(half, at):
        place = at * 4 + half * 2
        offset = pl.multiple_of(place * 128, 256)
        ref = hb if half is zh else hf
        value = jnp.concatenate([ref[at * 2].astype(F32), ref[at * 2 + 1].astype(F32)], axis=1)
        scaled = (value * again_ref[:, pl.ds(offset, 256)]).astype(BF)
        return value * value, scaled, offset

    wait_recv(hb.at[pl.ds(0, 7)], 0)
    squares = jnp.zeros((8, 256), F32)
    q_acc = jnp.zeros((8, 128), F32)
    g_acc = jnp.zeros((8, 128), F32)
    kv_acc = jnp.zeros((8, 128), F32)
    for i in range(4):
        square, scaled, offset = features(zh, i)
        squares = squares + square
        q_acc = q_acc + dot(scaled, wq[pl.ds(offset, 256), :])
        g_acc = g_acc + dot(scaled, wg[pl.ds(offset, 256), :])
        kv_acc = kv_acc + dot(scaled, wkv[pl.ds(offset, 256), :])
    wait_recv(hf, 1)
    rest = []
    for i in range(4):
        square, scaled, offset = features(oh, i)
        squares = squares + square
        rest.append((scaled, offset))
        q_acc = q_acc + dot(scaled, wq[pl.ds(offset, 256), :])
    row_scale = lax.rsqrt(jnp.sum(squares, axis=-1, keepdims=True) / WIDTH + EPS)
    query = normed_rotated(q_acc * row_scale, qgain_ref[...]).astype(BF)
    qs[...] = query
    qb[n] = query

    for dx, dc in FAR:
        send(qs, qf.at[n], 16, 3, (r, head_at(dx, 1, dc)))
    for dx, dc in NEAR:
        send(qs, qb.at[n], 1, 2, (r, head_at(dx, 0, dc)))

    wait_recv(wfar, 22)
    for dy in (2, 1, 3):
        send(wfar, wmlp.at[other_w], 8, 11, (ys_[dy] * 8 + z, h))
    kept = pltpu.make_async_copy(wfar, wmlp.at[other_w], lsem.at[21])
    kept.start()

    for scaled, offset in rest:
        g_acc = g_acc + dot(scaled, wg[pl.ds(offset, 256), :])
        kv_acc = kv_acc + dot(scaled, wkv[pl.ds(offset, 256), :])
    gate = jax.nn.sigmoid(g_acc * row_scale)
    projected = kv_acc * row_scale
    fresh = jnp.where(c == 0, normed_rotated(projected, kgain_ref[...]), projected).astype(BF)
    fs[...] = fresh
    fb[c] = fresh
    send(fs, fb.at[c], 2, 4, (r, head_at(0, 0, 1)))

    def attend(half, queries, sums):
        q = queries[...].astype(F32).reshape(64, 128).astype(BF)

        def weights(keys, live):
            scores = dot_nt(q, keys) * SCALE
            rows = lax.broadcasted_iota(jnp.int32, scores.shape, 0)
            cols = lax.broadcasted_iota(jnp.int32, scores.shape, 1)
            seen = ((cols & 7) == (rows >> 4) * 2 + half) & live(rows, cols)
            return jnp.where(seen, jnp.exp(scores), 0.0)

        def tail_live(rows, cols):
            limit = jnp.where(cols < 256, jnp.where(cols < 128, tails[0], tails[1]),
                              jnp.where(cols < 384, tails[2], tails[3])) - h * 16
            return ((cols >> 7) == ((rows & 7) >> 1)) & (((cols >> 3) & 15) < limit)

        w_prefix = weights(kc[pl.ds(0, 2048), :], lambda rows, cols: (cols >> 3) < plen - h * 256)
        w_tail = weights(kc[pl.ds(2048, 512), :], tail_live)
        numer = dot(w_prefix.astype(BF), vc[pl.ds(0, 2048), :]) + dot(w_tail.astype(BF), vc[pl.ds(2048, 512), :])
        total = jnp.sum(w_prefix, axis=-1, keepdims=True) + jnp.sum(w_tail, axis=-1, keepdims=True)
        high = total.astype(BF).astype(F32)
        lanes = lax.broadcasted_iota(jnp.int32, (64, 128), 1)
        totals = jnp.where(lanes < 64, high, total - high)
        both = jnp.concatenate([numer.reshape(8, 8, 128), totals.reshape(8, 8, 128)], axis=1)
        sums[...] = both.astype(BF)

    wait_recv(qb.at[pl.ds(0, 7)], 2)
    attend(zh, qb, mb)
    nb[n] = mb[n]
    for dx, dc in NEAR:
        send(mb.at[near_at(dx, dc)], nb.at[n], 3, 5, (r, head_at(dx, 0, dc)))
    wait_recv(qf, 3)
    attend(oh, qf, mf)
    for dx, dc in FAR:
        send(mf.at[near_at(dx, dc)], nf.at[n], 17, 6, (r, head_at(dx, 1, dc)))

    wait_recv(fb.at[0], 4)
    scores = dot_nt(query, fb[0]) * SCALE
    rows = lax.broadcasted_iota(jnp.int32, (8, 8), 0)
    cols = lax.broadcasted_iota(jnp.int32, (8, 8), 1)
    w_fresh = jnp.where((rows // 2 == cols // 2) & (cols <= rows), jnp.exp(scores), 0.0)
    numer = dot(w_fresh.astype(BF), fb[1])
    total = jnp.sum(w_fresh, axis=-1, keepdims=True)

    wait_recv(nb.at[pl.ds(0, 7)], 5)
    sums = jnp.sum(nb[...].astype(F32), axis=0)
    wait_recv(nf, 6)
    sums = sums + jnp.sum(nf[...].astype(F32), axis=0)
    numer = numer + sums[:8]
    total = total + sums[8:, 0:1] + sums[8:, 64:65]
    gated = (numer / total * gate).astype(BF)

    def quarter(low, high, odd):
        low = jnp.where(odd == 0, low, pltpu.roll(low, 64, 1))
        high = jnp.where(odd == 0, pltpu.roll(high, 64, 1), high)
        return jnp.where(lane < 64, low, high)

    mixed = dot(gated, wo[...])
    for place in range(8):
        px, pc = place // 2, place % 2
        for j in range(2):
            at = (2 * pc + j) * 512 + px * 64
            pieces = [mixed[:, at:at + 64], mixed[:, at + 256:at + 320]]
            sb[place, j] = jnp.concatenate(pieces, axis=1).astype(BF)
            block = 4 * px + 2 * j + pc
            sb[place, 2 + j] = mixed[:, block * 128:(block + 1) * 128].astype(BF)
    rb[n] = sb[n]
    for dx, dc in NEAR:
        send(sb.at[near_at(dx, dc)], rb.at[n], 4, 7, (r, head_at(dx, 0, dc)))
    wait_recv(rb.at[pl.ds(0, 7)], 7)
    sums = jnp.sum(rb[...].astype(F32), axis=0)
    first = jnp.where(zh == 0, 1.0, 0.0)

    for j in range(2):
        place = (2 * c + j) * 2 + lax.div(x, 2)
        tb[j] = (sums[j] + quarter(hb[place].astype(F32), hf[place].astype(F32), lax.rem(x, 2)) * first).astype(BF)
    residual = [sums[2] + hb[n].astype(F32) * first, sums[3] + hf[n].astype(F32) * first]

    slot = (zh * 4 + zq) * 2 + c
    target = y * 8 + zt * 4 + x
    pl.semaphore_wait(qsem, 3)
    for dz in (1, 0):
        for dx, dc in FAR:
            if dz or dx or dc:
                send(tb, xb.at[slot], 5, 8, (target, head_at(dx, dz, dc)))

    @pl.when(x != zq)
    def _():
        send(tb, xb.at[slot], 14, 8, (target, h))

        wait_recv(xb, 8)

    gains = []
    for fy in range(4):
        pair = []
        for i in range(2):
            offset = pl.multiple_of((fy * 4 + 2 * i + lax.div(zq, 2)) * 128, 128)
            pair.append(jnp.broadcast_to(mgain_ref[:, pl.ds(offset, 128)], (8, 128)))
        gains.append(quarter(*pair, lax.rem(zq, 2))[0:1])

    @pl.when(x == zq)
    def _():
        xb[slot] = tb[...]
        wait_recv(xb.at[pl.ds(0, 15)], 8)

    halves = xb[...].astype(F32)
    attended = halves[:8] + halves[8:]
    squares = jnp.zeros((32, 128), F32)
    parts = []
    for fy in range(4):
        block = jnp.concatenate([attended[i * 2 + fy // 2, fy % 2] for i in range(4)], axis=0)
        squares = squares + block * block
        parts.append((block * gains[fy]).astype(BF))
    mlp_in = jnp.concatenate(parts, axis=1)
    square = jnp.sum(squares, axis=-1, keepdims=True)
    high = square.astype(BF).astype(F32)
    lanes = lax.broadcasted_iota(jnp.int32, (32, 128), 1)
    square = jnp.where(lanes < 64, high, square - high)
    wait_recv(wmlp.at[pl.ds(0, 3)], 21)
    wait_recv(wmlp.at[pl.ds(0, 3)], 11)
    kept.wait()
    both = dot(mlp_in, wmlp[...].reshape(512, 768))

    for i in range(4):
        rows = slice(i * 8, i * 8 + 8)
        ps[i, :, 0:768] = both[rows].astype(BF)
        ps[i, :, 768:896] = square[rows].astype(BF)
    pb[zq] = ps[zq]
    for dzq in (2, 3, 1):
        to = zqs[dzq]
        send(ps.at[to], pb.at[zq], 6, 9, (y * 8 + zt * 4 + to, h))
    wait_recv(pb.at[pl.ds(0, 3)], 9)
    sums = jnp.sum(pb[...].astype(F32), axis=0)
    scale = lax.rsqrt((sums[:, 768:769] + sums[:, 832:833]) / WIDTH + EPS)
    act = (jax.nn.silu(sums[:, 0:384] * scale) * (sums[:, 384:768] * scale)).astype(BF)

    down = dot(act, wdown[...])
    for place in range(8):
        px, pc = place // 2, place % 2
        for j, block in enumerate((4 * px + pc, 4 * px + 2 + pc)):
            ds_[place, j] = down[:, block * 128:(block + 1) * 128].astype(BF)
    for j in range(2):
        ds_[n, j] = (ds_[n, j].astype(F32) + residual[j]).astype(BF)
    db[y * 8 + n] = ds_[n]
    for dy, dx, dc in SPREAD:
        send(ds_.at[near_at(dx, dc)], db.at[y * 8 + n], 7, 10, (ys_[dy] * 8 + z, head_at(dx, 0, dc)))
    wait_recv(db.at[pl.ds(0, 31)], 10)
    for i in range(4):
        yb[i] = jnp.sum(db[pl.ds(i * 8, 8)].astype(F32), axis=0).astype(BF)

    for i in range(8):
        zs[i] = yb[lax.div(owners[i], 8)]
    zb_[zh * 8 + z] = zs[z]
    for dz, dzl in [(1, 0)] + [(d, e) for e in (4, 3, 5, 2, 6, 1, 7) for d in (1, 0)]:
        to = zls[dzl]
        send(zs.at[to], zb_.at[zh * 8 + z], 9, 12, (y * 8 + to, head_at(0, dz, 0)))
    wait_recv(zb_.at[pl.ds(0, 15)], 12)
    wait_recv(gb.at[0], 20)
    from_z = lax.rem(owners[8], 8)
    final = (zb_[from_z].astype(F32) + zb_[8 + from_z].astype(F32)).astype(BF).astype(F32)
    out_ref[...] = jnp.where(zh == 0, final[0], final[1]).astype(BF)

    cs[0] = final[0] * final[0] + final[1] * final[1]
    cs[1] = final[0] * gb[0] + final[1] * gb[1]
    cb[n] = cs[...]
    for dx, dc in NEAR:
        send(cs, cb.at[n], 10, 13, (r, head_at(dx, 0, dc)))
    wait_recv(cb.at[pl.ds(0, 7)], 13)
    sums = jnp.sum(jnp.sum(cb[...], axis=0), axis=-1, keepdims=True)
    score = sums[1] * lax.rsqrt(sums[0] / WIDTH + EPS)
    score_ref[...] = jnp.sum(jnp.where(row == lane, score, 0.0), axis=0, keepdims=True)

    wait_send(hb.at[pl.ds(0, 7)], 0)
    wait_send(hf, 15)
    wait_send(qb.at[pl.ds(0, 7)], 1)
    wait_send(qf, 16)
    wait_send(fb.at[0], 2)
    wait_send(nb.at[pl.ds(0, 7)], 3)
    wait_send(nf, 17)
    wait_send(rb.at[pl.ds(0, 7)], 4)
    wait_send(xb.at[pl.ds(0, 15)], 5)

    @pl.when(x != zq)
    def _():
        wait_send(xb.at[0], 14)
    wait_send(pb.at[pl.ds(0, 3)], 6)
    wait_send(db.at[pl.ds(0, 31)], 7)
    wait_send(zb_.at[pl.ds(0, 15)], 9)
    wait_send(cb.at[pl.ds(0, 7)], 10)
    wait_send(gb.at[0], 11)
    wait_send(wmlp.at[pl.ds(0, 3)], 12)
    wait_send(wmlp.at[0], 13)
    wait_send(wmlp.at[pl.ds(0, 3)], 8)


def hand_over(out_from, score_from, out_ref, score_ref):
    out_ref[...] = out_from[...]
    score_ref[...] = score_from[:, 0:8]


def shards(
    hidden, attn_gain, q_weight, gate_weight, key_value_weight, q_gain, k_gain, out_weight,
    prompt_key_cache, prompt_value_cache, tail_key_cache, tail_value_cache, mlp_gain, mlp_gate,
    mlp_up, mlp_down, final_gain, score_weight, prompt_lengths, tail_lengths, group_prompt,
):
    vmem = pl.BlockSpec(memory_space=pltpu.VMEM)
    hbm = pl.BlockSpec(memory_space=pl.ANY)

    def blocks(*shape, kind=BF):
        return pltpu.VMEM(shape, kind)

    out, score = pl.pallas_call(
        kernel,
        out_shape=(jax.ShapeDtypeStruct((8, 128), BF), jax.ShapeDtypeStruct((1, 128), F32)),
        in_specs=[hbm] * 21,
        out_specs=(vmem, vmem),
        scratch_shapes=[
            pltpu.SMEM((32,), jnp.int32), pltpu.SMEM((4, 32), jnp.int32), pltpu.SMEM((32,), jnp.int32),
            blocks(1, 2048, kind=F32), blocks(1, 128, kind=F32), blocks(1, 128, kind=F32),
            blocks(1, 2048, kind=F32), blocks(1, 128, kind=F32), blocks(1, 128, kind=F32),
            blocks(2048, 128), blocks(2048, 128), blocks(2048, 128), blocks(128, 2048),
            blocks(2560, 128), blocks(2560, 128),
            blocks(8, 64, 768), blocks(64, 768), blocks(384, 2048),
            blocks(8, 8, 128), blocks(8, 8, 128),
            blocks(8, 128), blocks(8, 8, 128), blocks(8, 8, 128),
            blocks(8, 128), blocks(2, 8, 128),
            blocks(8, 16, 128), blocks(8, 16, 128),
            blocks(8, 16, 128), blocks(8, 16, 128),
            blocks(8, 4, 8, 128), blocks(8, 4, 8, 128),
            blocks(2, 8, 128), blocks(16, 2, 8, 128),
            blocks(4, 8, 896), blocks(4, 8, 896),
            blocks(8, 2, 8, 128), blocks(32, 2, 8, 128),
            blocks(4, 2, 8, 128),
            blocks(8, 2, 8, 128), blocks(16, 2, 8, 128),
            blocks(2, 8, 128, kind=F32), blocks(8, 2, 8, 128, kind=F32),
            blocks(8, 128, kind=F32), blocks(2, 8, 128, kind=F32),
            pltpu.SemaphoreType.DMA((22,)),
            pltpu.SemaphoreType.DMA((18,)),
            pltpu.SemaphoreType.DMA((23,)),
            pltpu.SemaphoreType.REGULAR,
        ],
        compiler_params=pltpu.CompilerParams(
            collective_id=0, has_side_effects=True, vmem_limit_bytes=60 << 20
        ),
    )(
        prompt_lengths, tail_lengths.T, group_prompt,
        hidden, attn_gain.reshape(1, -1), q_gain.reshape(1, -1), k_gain.reshape(1, -1),
        mlp_gain.reshape(1, -1), final_gain.reshape(1, -1), score_weight.reshape(1, -1),
        q_weight, gate_weight, key_value_weight, out_weight,
        prompt_key_cache.reshape(-1, 128), prompt_value_cache.reshape(-1, 128),
        tail_key_cache.reshape(-1, 128), tail_value_cache.reshape(-1, 128),
        mlp_gate, mlp_up, mlp_down,
    )
    out, score = pl.pallas_call(
        hand_over,
        out_shape=(jax.ShapeDtypeStruct((8, 128), BF), jax.ShapeDtypeStruct((1, 8), F32)),
        in_specs=[vmem] * 2,
        out_specs=(vmem, vmem),
    )(out, score)
    return out, score[0]


def solution(mesh):
    return jax.shard_map(
        shards,
        mesh=mesh,
        in_specs=(
            P("req", "head"),
            P(),
            P(None, "head"),
            P(None, "head"),
            P(None, "head"),
            P(),
            P(),
            P("head", None),
            P("req", "head", None, None),
            P("req", "head", None, None),
            P("req", None, "head", None, None),
            P("req", None, "head", None, None),
            P(),
            P("req", "head"),
            P("req", "head"),
            P("head", None),
            P("head"),
            P("head"),
            P(),
            P(),
            P(),
        ),
        out_specs=(P("req", "head"), P("req")),
        check_vma=False,
    )
```

```python
import math

import jax
import jax.numpy as jnp
from jax import lax
from jax.experimental import pallas as pl
from jax.experimental.pallas import tpu as pltpu
from jax.sharding import PartitionSpec as P

EPS = 1e-06
THETA = 1000000.0
MESH = pl.DeviceIdType.MESH
BF = jnp.bfloat16
F32 = jnp.float32
WIDTH = 2048
SCALE = 1.0 / math.sqrt(128.0)

NEAR = [(2, 1), (2, 0), (1, 1), (3, 1), (1, 0), (3, 0), (0, 1)]
FAR = [(2, 1), (2, 0), (1, 1), (3, 1), (1, 0), (3, 0), (0, 1), (0, 0)]

SPREAD = sorted(
    ((dy, dx, dc) for dy in range(4) for dx in range(4) for dc in range(2) if dy or dx or dc),
    key=lambda at: -(min(at[0], 4 - at[0]) + min(at[1], 4 - at[1]) + at[2] * 0.5),
)

RING = [(1, 0), (1, 1), (1, 7), (1, 2), (1, 6), (0, 4), (1, 3), (1, 5), (0, 3), (0, 5), (1, 4), (0, 2), (0, 6), (0, 1), (0, 7)]


def dot(a, b):
    return jnp.dot(a, b, preferred_element_type=F32)


def dot_nt(a, b):
    return lax.dot_general(a, b, (((1,), (1,)), ((), ())), preferred_element_type=F32)


def kernel(
    plen_hbm, tlen_hbm, gp_hbm, hidden_hbm, again_hbm, qgain_hbm, kgain_hbm, mgain_hbm, fgain_hbm, sw_hbm,
    wq_hbm, wg_hbm, wkv_hbm, wo_hbm, pk_hbm, pv_hbm, tk_hbm, tv_hbm, mg_hbm, mu_hbm, md_hbm,
    out_ref, score_ref,
    plen_ref, tlen_ref, gp_ref, again_ref, qgain_ref, kgain_ref, mgain_ref, fgain_ref, sw_ref,
    wq, wg, wkv, wo, kc, vc, wmlp, wfar, wdown,
    hb, hf, qs, qb, qf, fs, fb, mb, mf, nb, nf, sb, rb, tb, xb, ps, pb, ds_, db, yb, zs, zb_, cs, cb, gs, gb,
    lsem, ssem, rsem, qsem,
):
    r = lax.axis_index("req")
    h = lax.axis_index("head")
    y, z = lax.div(r, 8), lax.rem(r, 8)
    x, zh, c = lax.div(h, 4), lax.rem(lax.div(h, 2), 2), lax.rem(h, 2)
    zt, zq = lax.div(z, 4), lax.rem(z, 4)
    n = x * 2 + c
    oh = 1 - zh

    def around(value, size):
        shifted = [value] + [value + i for i in range(1, size)]
        return [jnp.where(v >= size, v - size, v) for v in shifted]

    xs, ys_, zqs, zls = around(x, 4), around(y, 4), around(zq, 4), around(z, 8)
    zhs, cc = around(zh, 2), around(c, 2)
    own_w, other_w = y * 2 + zt, y * 2 + 1 - zt
    across = (y * 8 + (1 - zt) * 4 + zq, h)

    def head_at(dx, dz, dc):
        return xs[dx] * 4 + zhs[dz] * 2 + cc[dc]

    def near_at(dx, dc):
        return xs[dx] * 2 + cc[dc]

    def send(src, dst, phase, at, dev):
        pltpu.make_async_remote_copy(
            src_ref=src, dst_ref=dst, send_sem=ssem.at[phase], recv_sem=rsem.at[at],
            device_id=dev, device_id_type=MESH,
        ).start()

    def waiter(ref, phase, at):
        return pltpu.make_async_remote_copy(
            src_ref=ref, dst_ref=ref, send_sem=ssem.at[phase], recv_sem=rsem.at[at],
            device_id=(r, head_at(0, 0, 1)), device_id_type=MESH,
        )

    def wait_recv(ref, at):
        waiter(ref, 0, at).wait_recv()

    def wait_send(ref, phase):
        waiter(ref, phase, 0).wait_send()

    hidden_copy = pltpu.make_async_copy(hidden_hbm, hb.at[n], lsem.at[0])
    hidden_copy.start()
    bar = pltpu.get_barrier_semaphore()

    def greet(dev):
        pl.semaphore_signal(bar, inc=1, device_id=dev, device_id_type=MESH)

    for dx, dc in FAR:
        greet((r, head_at(dx, 1, dc)))
    greet(across)
    for dzq in (2, 3, 1):
        greet((y * 8 + zt * 4 + zqs[dzq], h))
    for dy in (2, 1, 3):
        greet((ys_[dy] * 8 + z, h))
    for dx, dc in NEAR:
        greet((r, head_at(dx, 0, dc)))

    local = [
        (mg_hbm, wmlp.at[own_w, :, pl.ds(0, 384)]), (mu_hbm, wmlp.at[own_w, :, pl.ds(384, 384)]),
        (fgain_hbm, fgain_ref), (sw_hbm, sw_ref), (plen_hbm, plen_ref), (tlen_hbm, tlen_ref), (gp_hbm, gp_ref),
        (again_hbm, again_ref), (wq_hbm, wq), (qgain_hbm, qgain_ref), (kgain_hbm, kgain_ref),
        (wg_hbm, wg), (wkv_hbm, wkv),
        (pk_hbm, kc.at[pl.ds(0, 2048)]), (tk_hbm, kc.at[pl.ds(2048, 512)]),
        (pv_hbm, vc.at[pl.ds(0, 2048)]), (tv_hbm, vc.at[pl.ds(2048, 512)]),
        (wo_hbm, wo), (mgain_hbm, mgain_ref), (md_hbm, wdown),
    ]
    copies = [pltpu.make_async_copy(s, d, lsem.at[i + 1]) for i, (s, d) in enumerate(local)]
    for cp in copies:
        cp.start()
    hidden_copy.wait()
    pl.semaphore_wait(bar, 22)

    for dx, dc in FAR:
        send(hb.at[n], hf.at[n], 15, 1, (r, head_at(dx, 1, dc)))
    for dx, dc in NEAR:
        send(hb.at[n], hb.at[n], 0, 0, (r, head_at(dx, 0, dc)))

    copies[0].wait()
    copies[1].wait()
    send(wmlp.at[own_w], wfar, 13, 22, across)
    for dy in (2, 1, 3):
        send(wmlp.at[own_w], wmlp.at[own_w], 12, 21, (ys_[dy] * 8 + z, h))
    for dzq in (2, 3, 1):
        pl.semaphore_signal(qsem, inc=1, device_id=(y * 8 + zt * 4 + zqs[dzq], h), device_id_type=MESH)
    for i in range(2, 20):
        copies[i].wait()
    gs[...] = jnp.broadcast_to(fgain_ref[...] * sw_ref[...], (8, 128))
    gb[zh] = gs[...]
    send(gs, gb.at[zh], 11, 20, (r, head_at(0, 1, 0)))

    prompt = gp_ref[r]
    plen = plen_ref[prompt]
    tails = [tlen_ref[i, prompt] for i in range(4)]

    def find(g, found):
        value = gp_ref[g]
        mine = jnp.where(value == r, g, found[8])
        return tuple(jnp.where(value == y * 8 + i, g, found[i]) for i in range(8)) + (mine,)

    owners = lax.fori_loop(0, 32, find, (jnp.int32(0),) * 9)

    row = lax.broadcasted_iota(jnp.int32, (8, 128), 0)
    lane = lax.broadcasted_iota(jnp.int32, (8, 128), 1)
    position = plen + row % 2
    for i in range(4):
        position = position + jnp.where(row // 2 == i, tails[i], 0)
    half_lane = (lane % 64).astype(F32)
    frequency = jnp.exp(-math.log(THETA) * 2.0 * half_lane / 128.0)
    angle = position.astype(F32) * frequency
    cosine = jnp.cos(angle)
    sine = jnp.sin(angle)
    sine = jnp.where(lane < 64, -sine, sine)

    def normed_rotated(value, gain):
        value = value * lax.rsqrt(jnp.mean(value * value, axis=-1, keepdims=True) + EPS) * gain
        return value * cosine + pltpu.roll(value, 64, 1) * sine

    def features(half, at):
        place = at * 4 + half * 2
        offset = pl.multiple_of(place * 128, 256)
        ref = hb if half is zh else hf
        value = jnp.concatenate([ref[at * 2].astype(F32), ref[at * 2 + 1].astype(F32)], axis=1)
        scaled = (value * again_ref[:, pl.ds(offset, 256)]).astype(BF)
        return value * value, scaled, offset

    wait_recv(hb.at[pl.ds(0, 7)], 0)
    squares = jnp.zeros((8, 256), F32)
    q_acc = jnp.zeros((8, 128), F32)
    g_acc = jnp.zeros((8, 128), F32)
    kv_acc = jnp.zeros((8, 128), F32)
    for i in range(4):
        square, scaled, offset = features(zh, i)
        squares = squares + square
        q_acc = q_acc + dot(scaled, wq[pl.ds(offset, 256), :])
        g_acc = g_acc + dot(scaled, wg[pl.ds(offset, 256), :])
        kv_acc = kv_acc + dot(scaled, wkv[pl.ds(offset, 256), :])
    wait_recv(hf, 1)
    rest = []
    for i in range(4):
        square, scaled, offset = features(oh, i)
        squares = squares + square
        rest.append((scaled, offset))
        q_acc = q_acc + dot(scaled, wq[pl.ds(offset, 256), :])
    row_scale = lax.rsqrt(jnp.sum(squares, axis=-1, keepdims=True) / WIDTH + EPS)
    query = normed_rotated(q_acc * row_scale, qgain_ref[...]).astype(BF)
    qs[...] = query
    qb[n] = query

    for dx, dc in FAR:
        send(qs, qf.at[n], 16, 3, (r, head_at(dx, 1, dc)))
    for dx, dc in NEAR:
        send(qs, qb.at[n], 1, 2, (r, head_at(dx, 0, dc)))

    wait_recv(wfar, 22)
    for dy in (2, 1, 3):
        send(wfar, wmlp.at[other_w], 8, 11, (ys_[dy] * 8 + z, h))
    kept = pltpu.make_async_copy(wfar, wmlp.at[other_w], lsem.at[21])
    kept.start()

    for scaled, offset in rest:
        g_acc = g_acc + dot(scaled, wg[pl.ds(offset, 256), :])
        kv_acc = kv_acc + dot(scaled, wkv[pl.ds(offset, 256), :])
    gate = jax.nn.sigmoid(g_acc * row_scale)
    projected = kv_acc * row_scale
    fresh = jnp.where(c == 0, normed_rotated(projected, kgain_ref[...]), projected).astype(BF)
    fs[...] = fresh
    fb[c] = fresh
    send(fs, fb.at[c], 2, 4, (r, head_at(0, 0, 1)))

    def attend(half, queries, sums):
        q = queries[...].astype(F32).reshape(64, 128).astype(BF)

        def weights(keys, live):
            scores = dot_nt(q, keys) * SCALE
            rows = lax.broadcasted_iota(jnp.int32, scores.shape, 0)
            cols = lax.broadcasted_iota(jnp.int32, scores.shape, 1)
            seen = ((cols & 7) == (rows >> 4) * 2 + half) & live(rows, cols)
            return jnp.where(seen, jnp.exp(scores), 0.0)

        def tail_live(rows, cols):
            limit = jnp.where(cols < 256, jnp.where(cols < 128, tails[0], tails[1]),
                              jnp.where(cols < 384, tails[2], tails[3])) - h * 16
            return ((cols >> 7) == ((rows & 7) >> 1)) & (((cols >> 3) & 15) < limit)

        w_prefix = weights(kc[pl.ds(0, 2048), :], lambda rows, cols: (cols >> 3) < plen - h * 256)
        w_tail = weights(kc[pl.ds(2048, 512), :], tail_live)
        numer = dot(w_prefix.astype(BF), vc[pl.ds(0, 2048), :]) + dot(w_tail.astype(BF), vc[pl.ds(2048, 512), :])
        total = jnp.sum(w_prefix, axis=-1, keepdims=True) + jnp.sum(w_tail, axis=-1, keepdims=True)
        high = total.astype(BF).astype(F32)
        lanes = lax.broadcasted_iota(jnp.int32, (64, 128), 1)
        totals = jnp.where(lanes < 64, high, total - high)
        both = jnp.concatenate([numer.reshape(8, 8, 128), totals.reshape(8, 8, 128)], axis=1)
        sums[...] = both.astype(BF)

    wait_recv(qb.at[pl.ds(0, 7)], 2)
    attend(zh, qb, mb)
    nb[n] = mb[n]
    for dx, dc in NEAR:
        send(mb.at[near_at(dx, dc)], nb.at[n], 3, 5, (r, head_at(dx, 0, dc)))
    wait_recv(qf, 3)
    attend(oh, qf, mf)
    for dx, dc in FAR:
        send(mf.at[near_at(dx, dc)], nf.at[n], 17, 6, (r, head_at(dx, 1, dc)))

    wait_recv(fb.at[0], 4)
    scores = dot_nt(query, fb[0]) * SCALE
    rows = lax.broadcasted_iota(jnp.int32, (8, 8), 0)
    cols = lax.broadcasted_iota(jnp.int32, (8, 8), 1)
    w_fresh = jnp.where((rows // 2 == cols // 2) & (cols <= rows), jnp.exp(scores), 0.0)
    numer = dot(w_fresh.astype(BF), fb[1])
    total = jnp.sum(w_fresh, axis=-1, keepdims=True)

    wait_recv(nb.at[pl.ds(0, 7)], 5)
    sums = jnp.sum(nb[...].astype(F32), axis=0)
    wait_recv(nf, 6)
    sums = sums + jnp.sum(nf[...].astype(F32), axis=0)
    numer = numer + sums[:8]
    total = total + sums[8:, 0:1] + sums[8:, 64:65]
    gated = (numer / total * gate).astype(BF)

    def quarter(low, high, odd):
        low = jnp.where(odd == 0, low, pltpu.roll(low, 64, 1))
        high = jnp.where(odd == 0, pltpu.roll(high, 64, 1), high)
        return jnp.where(lane < 64, low, high)

    mixed = dot(gated, wo[...])
    for place in range(8):
        px, pc = place // 2, place % 2
        for j in range(2):
            at = (2 * pc + j) * 512 + px * 64
            pieces = [mixed[:, at:at + 64], mixed[:, at + 256:at + 320]]
            sb[place, j] = jnp.concatenate(pieces, axis=1).astype(BF)
            block = 4 * px + 2 * j + pc
            sb[place, 2 + j] = mixed[:, block * 128:(block + 1) * 128].astype(BF)
    rb[n] = sb[n]
    for dx, dc in NEAR:
        send(sb.at[near_at(dx, dc)], rb.at[n], 4, 7, (r, head_at(dx, 0, dc)))
    wait_recv(rb.at[pl.ds(0, 7)], 7)
    sums = jnp.sum(rb[...].astype(F32), axis=0)
    first = jnp.where(zh == 0, 1.0, 0.0)

    for j in range(2):
        place = (2 * c + j) * 2 + lax.div(x, 2)
        tb[j] = (sums[j] + quarter(hb[place].astype(F32), hf[place].astype(F32), lax.rem(x, 2)) * first).astype(BF)
    residual = [sums[2] + hb[n].astype(F32) * first, sums[3] + hf[n].astype(F32) * first]

    slot = (zh * 4 + zq) * 2 + c
    target = y * 8 + zt * 4 + x
    pl.semaphore_wait(qsem, 3)
    for dz in (1, 0):
        for dx, dc in FAR:
            if dz or dx or dc:
                send(tb, xb.at[slot], 5, 8, (target, head_at(dx, dz, dc)))

    @pl.when(x != zq)
    def _():
        send(tb, xb.at[slot], 14, 8, (target, h))

        wait_recv(xb, 8)

    gains = []
    for fy in range(4):
        pair = []
        for i in range(2):
            offset = pl.multiple_of((fy * 4 + 2 * i + lax.div(zq, 2)) * 128, 128)
            pair.append(jnp.broadcast_to(mgain_ref[:, pl.ds(offset, 128)], (8, 128)))
        gains.append(quarter(*pair, lax.rem(zq, 2))[0:1])

    @pl.when(x == zq)
    def _():
        xb[slot] = tb[...]
        wait_recv(xb.at[pl.ds(0, 15)], 8)

    halves = xb[...].astype(F32)
    attended = halves[:8] + halves[8:]
    squares = jnp.zeros((32, 128), F32)
    parts = []
    for fy in range(4):
        block = jnp.concatenate([attended[i * 2 + fy // 2, fy % 2] for i in range(4)], axis=0)
        squares = squares + block * block
        parts.append((block * gains[fy]).astype(BF))
    mlp_in = jnp.concatenate(parts, axis=1)
    square = jnp.sum(squares, axis=-1, keepdims=True)
    high = square.astype(BF).astype(F32)
    lanes = lax.broadcasted_iota(jnp.int32, (32, 128), 1)
    square = jnp.where(lanes < 64, high, square - high)
    wait_recv(wmlp.at[pl.ds(0, 3)], 21)
    wait_recv(wmlp.at[pl.ds(0, 3)], 11)
    kept.wait()
    both = dot(mlp_in, wmlp[...].reshape(512, 768))

    for i in range(4):
        rows = slice(i * 8, i * 8 + 8)
        ps[i, :, 0:768] = both[rows].astype(BF)
        ps[i, :, 768:896] = square[rows].astype(BF)
    pb[zq] = ps[zq]
    for dzq in (2, 3, 1):
        to = zqs[dzq]
        send(ps.at[to], pb.at[zq], 6, 9, (y * 8 + zt * 4 + to, h))
    wait_recv(pb.at[pl.ds(0, 3)], 9)
    sums = jnp.sum(pb[...].astype(F32), axis=0)
    scale = lax.rsqrt((sums[:, 768:769] + sums[:, 832:833]) / WIDTH + EPS)
    act = (jax.nn.silu(sums[:, 0:384] * scale) * (sums[:, 384:768] * scale)).astype(BF)

    down = dot(act, wdown[...])
    for place in range(8):
        px, pc = place // 2, place % 2
        for j, block in enumerate((4 * px + pc, 4 * px + 2 + pc)):
            ds_[place, j] = down[:, block * 128:(block + 1) * 128].astype(BF)
    for j in range(2):
        ds_[n, j] = (ds_[n, j].astype(F32) + residual[j]).astype(BF)
    db[y * 8 + n] = ds_[n]
    for dy, dx, dc in SPREAD:
        send(ds_.at[near_at(dx, dc)], db.at[y * 8 + n], 7, 10, (ys_[dy] * 8 + z, head_at(dx, 0, dc)))
    wait_recv(db.at[pl.ds(0, 31)], 10)
    for i in range(4):
        yb[i] = jnp.sum(db[pl.ds(i * 8, 8)].astype(F32), axis=0).astype(BF)

    for i in range(8):
        zs[i] = yb[lax.div(owners[i], 8)]
    zb_[zh * 8 + z] = zs[z]
    for dz, dzl in RING:
        to = zls[dzl]
        send(zs.at[to], zb_.at[zh * 8 + z], 9, 12, (y * 8 + to, head_at(0, dz, 0)))
    wait_recv(zb_.at[pl.ds(0, 15)], 12)
    wait_recv(gb.at[0], 20)
    from_z = lax.rem(owners[8], 8)
    final = (zb_[from_z].astype(F32) + zb_[8 + from_z].astype(F32)).astype(BF).astype(F32)
    out_ref[...] = jnp.where(zh == 0, final[0], final[1]).astype(BF)

    cs[0] = final[0] * final[0] + final[1] * final[1]
    cs[1] = final[0] * gb[0] + final[1] * gb[1]
    cb[n] = cs[...]
    for dx, dc in NEAR:
        send(cs, cb.at[n], 10, 13, (r, head_at(dx, 0, dc)))
    wait_recv(cb.at[pl.ds(0, 7)], 13)
    sums = jnp.sum(jnp.sum(cb[...], axis=0), axis=-1, keepdims=True)
    score = sums[1] * lax.rsqrt(sums[0] / WIDTH + EPS)
    score_ref[...] = jnp.sum(jnp.where(row == lane, score, 0.0), axis=0, keepdims=True)

    wait_send(hb.at[pl.ds(0, 7)], 0)
    wait_send(hf, 15)
    wait_send(qb.at[pl.ds(0, 7)], 1)
    wait_send(qf, 16)
    wait_send(fb.at[0], 2)
    wait_send(nb.at[pl.ds(0, 7)], 3)
    wait_send(nf, 17)
    wait_send(rb.at[pl.ds(0, 7)], 4)
    wait_send(xb.at[pl.ds(0, 15)], 5)

    @pl.when(x != zq)
    def _():
        wait_send(xb.at[0], 14)
    wait_send(pb.at[pl.ds(0, 3)], 6)
    wait_send(db.at[pl.ds(0, 31)], 7)
    wait_send(zb_.at[pl.ds(0, 15)], 9)
    wait_send(cb.at[pl.ds(0, 7)], 10)
    wait_send(gb.at[0], 11)
    wait_send(wmlp.at[pl.ds(0, 3)], 12)
    wait_send(wmlp.at[0], 13)
    wait_send(wmlp.at[pl.ds(0, 3)], 8)


def shards(
    hidden, attn_gain, q_weight, gate_weight, key_value_weight, q_gain, k_gain, out_weight,
    prompt_key_cache, prompt_value_cache, tail_key_cache, tail_value_cache, mlp_gain, mlp_gate,
    mlp_up, mlp_down, final_gain, score_weight, prompt_lengths, tail_lengths, group_prompt,
):
    vmem = pl.BlockSpec(memory_space=pltpu.VMEM)
    hbm = pl.BlockSpec(memory_space=pl.ANY)

    def blocks(*shape, kind=BF):
        return pltpu.VMEM(shape, kind)

    out, score = pl.pallas_call(
        kernel,
        out_shape=(pltpu.VMEM((8, 128), BF), pltpu.VMEM((1, 128), F32)),
        in_specs=[hbm] * 21,
        out_specs=(vmem, vmem),
        scratch_shapes=[
            pltpu.SMEM((32,), jnp.int32), pltpu.SMEM((4, 32), jnp.int32), pltpu.SMEM((32,), jnp.int32),
            blocks(1, 2048, kind=F32), blocks(1, 128, kind=F32), blocks(1, 128, kind=F32),
            blocks(1, 2048, kind=F32), blocks(1, 128, kind=F32), blocks(1, 128, kind=F32),
            blocks(2048, 128), blocks(2048, 128), blocks(2048, 128), blocks(128, 2048),
            blocks(2560, 128), blocks(2560, 128),
            blocks(8, 64, 768), blocks(64, 768), blocks(384, 2048),
            blocks(8, 8, 128), blocks(8, 8, 128),
            blocks(8, 128), blocks(8, 8, 128), blocks(8, 8, 128),
            blocks(8, 128), blocks(2, 8, 128),
            blocks(8, 16, 128), blocks(8, 16, 128),
            blocks(8, 16, 128), blocks(8, 16, 128),
            blocks(8, 4, 8, 128), blocks(8, 4, 8, 128),
            blocks(2, 8, 128), blocks(16, 2, 8, 128),
            blocks(4, 8, 896), blocks(4, 8, 896),
            blocks(8, 2, 8, 128), blocks(32, 2, 8, 128),
            blocks(4, 2, 8, 128),
            blocks(8, 2, 8, 128), blocks(16, 2, 8, 128),
            blocks(2, 8, 128, kind=F32), blocks(8, 2, 8, 128, kind=F32),
            blocks(8, 128, kind=F32), blocks(2, 8, 128, kind=F32),
            pltpu.SemaphoreType.DMA((22,)),
            pltpu.SemaphoreType.DMA((18,)),
            pltpu.SemaphoreType.DMA((23,)),
            pltpu.SemaphoreType.REGULAR,
        ],
        compiler_params=pltpu.CompilerParams(
            collective_id=0, has_side_effects=True, vmem_limit_bytes=60 << 20
        ),
    )(
        prompt_lengths, tail_lengths.T, group_prompt,
        hidden, attn_gain.reshape(1, -1), q_gain.reshape(1, -1), k_gain.reshape(1, -1),
        mlp_gain.reshape(1, -1), final_gain.reshape(1, -1), score_weight.reshape(1, -1),
        q_weight, gate_weight, key_value_weight, out_weight,
        prompt_key_cache.reshape(-1, 128), prompt_value_cache.reshape(-1, 128),
        tail_key_cache.reshape(-1, 128), tail_value_cache.reshape(-1, 128),
        mlp_gate, mlp_up, mlp_down,
    )
    return out, score[0, :8]


def solution(mesh):
    return jax.shard_map(
        shards,
        mesh=mesh,
        in_specs=(
            P("req", "head"),
            P(),
            P(None, "head"),
            P(None, "head"),
            P(None, "head"),
            P(),
            P(),
            P("head", None),
            P("req", "head", None, None),
            P("req", "head", None, None),
            P("req", None, "head", None, None),
            P("req", None, "head", None, None),
            P(),
            P("req", "head"),
            P("req", "head"),
            P("head", None),
            P("head"),
            P("head"),
            P(),
            P(),
            P(),
        ),
        out_specs=(P("req", "head"), P("req")),
        check_vma=False,
    )
```

```python
import math

import jax
import jax.numpy as jnp
from jax import lax
from jax.experimental import pallas as pl
from jax.experimental.pallas import tpu as pltpu
from jax.sharding import PartitionSpec as P

EPS = 1e-06
THETA = 1000000.0
MESH = pl.DeviceIdType.MESH
BF = jnp.bfloat16
F32 = jnp.float32
WIDTH = 2048
SCALE = 1.0 / math.sqrt(128.0)

NEAR = [(2, 1), (2, 0), (1, 1), (3, 1), (1, 0), (3, 0), (0, 1)]
FAR = [(2, 1), (2, 0), (1, 1), (3, 1), (1, 0), (3, 0), (0, 1), (0, 0)]

SPREAD = sorted(
    ((dy, dx, dc) for dy in range(4) for dx in range(4) for dc in range(2) if dy or dx or dc),
    key=lambda at: -(min(at[0], 4 - at[0]) + min(at[1], 4 - at[1]) + at[2] * 0.5),
)

RING = [(1, 0), (1, 1), (1, 7), (1, 2), (1, 6), (0, 4), (1, 3), (1, 5), (0, 3), (0, 5), (1, 4), (0, 2), (0, 6), (0, 1), (0, 7)]


def dot(a, b):
    return jnp.dot(a, b, preferred_element_type=F32)


def dot_nt(a, b):
    return lax.dot_general(a, b, (((1,), (1,)), ((), ())), preferred_element_type=F32)


def kernel(
    plen_hbm, tlen_hbm, gp_hbm, hidden_hbm, again_hbm, qgain_hbm, kgain_hbm, mgain_hbm, fgain_hbm, sw_hbm,
    wq_hbm, wg_hbm, wkv_hbm, wo_hbm, pk_hbm, pv_hbm, tk_hbm, tv_hbm, mg_hbm, mu_hbm, md_hbm,
    out_ref, score_ref,
    plen_ref, tlen_ref, gp_ref, again_ref, qgain_ref, kgain_ref, mgain_ref, fgain_ref, sw_ref,
    wq, wg, wkv, wo, kc, kt, vc, wmlp, wfar, wdown,
    hb, hf, qs, qb, qf, fs, fb, mb, mf, nb, nf, sb, rb, tb, xb, ps, pb, ds_, db, yb, zs, zb_, cs, cb, gs, gb,
    lsem, ssem, rsem, qsem,
):
    r = lax.axis_index("req")
    h = lax.axis_index("head")
    y, z = lax.div(r, 8), lax.rem(r, 8)
    x, zh, c = lax.div(h, 4), lax.rem(lax.div(h, 2), 2), lax.rem(h, 2)
    zt, zq = lax.div(z, 4), lax.rem(z, 4)
    n = x * 2 + c
    oh = 1 - zh

    def around(value, size):
        shifted = [value] + [value + i for i in range(1, size)]
        return [jnp.where(v >= size, v - size, v) for v in shifted]

    xs, ys_, zqs, zls = around(x, 4), around(y, 4), around(zq, 4), around(z, 8)
    zhs, cc = around(zh, 2), around(c, 2)
    own_w, other_w = y * 2 + zt, y * 2 + 1 - zt
    across = (y * 8 + (1 - zt) * 4 + zq, h)

    def head_at(dx, dz, dc):
        return xs[dx] * 4 + zhs[dz] * 2 + cc[dc]

    def near_at(dx, dc):
        return xs[dx] * 2 + cc[dc]

    def send(src, dst, phase, at, dev):
        pltpu.make_async_remote_copy(
            src_ref=src, dst_ref=dst, send_sem=ssem.at[phase], recv_sem=rsem.at[at],
            device_id=dev, device_id_type=MESH,
        ).start()

    def waiter(ref, phase, at):
        return pltpu.make_async_remote_copy(
            src_ref=ref, dst_ref=ref, send_sem=ssem.at[phase], recv_sem=rsem.at[at],
            device_id=(r, head_at(0, 0, 1)), device_id_type=MESH,
        )

    def wait_recv(ref, at):
        waiter(ref, 0, at).wait_recv()

    def wait_send(ref, phase):
        waiter(ref, phase, 0).wait_send()

    hidden_copy = pltpu.make_async_copy(hidden_hbm, hb.at[n], lsem.at[0])
    hidden_copy.start()
    bar = pltpu.get_barrier_semaphore()

    def greet(dev):
        pl.semaphore_signal(bar, inc=1, device_id=dev, device_id_type=MESH)

    for dx, dc in FAR:
        greet((r, head_at(dx, 1, dc)))
    greet(across)
    for dzq in (2, 3, 1):
        greet((y * 8 + zt * 4 + zqs[dzq], h))
    for dy in (2, 1, 3):
        greet((ys_[dy] * 8 + z, h))
    for dx, dc in NEAR:
        greet((r, head_at(dx, 0, dc)))

    local = [
        (mg_hbm, wmlp.at[own_w, :, pl.ds(0, 384)]), (mu_hbm, wmlp.at[own_w, :, pl.ds(384, 384)]),
        (fgain_hbm, fgain_ref), (sw_hbm, sw_ref), (plen_hbm, plen_ref), (tlen_hbm, tlen_ref), (gp_hbm, gp_ref),
        (again_hbm, again_ref), (wq_hbm, wq), (qgain_hbm, qgain_ref), (kgain_hbm, kgain_ref),
        (wg_hbm, wg), (wkv_hbm, wkv),
        (pk_hbm, kc.at[pl.ds(0, 2048)]), (tk_hbm, kc.at[pl.ds(2048, 512)]),
        (pv_hbm, vc.at[pl.ds(0, 2048)]), (tv_hbm, vc.at[pl.ds(2048, 512)]),
        (wo_hbm, wo), (mgain_hbm, mgain_ref), (md_hbm, wdown),
    ]
    copies = [pltpu.make_async_copy(s, d, lsem.at[i + 1]) for i, (s, d) in enumerate(local)]
    for cp in copies:
        cp.start()
    hidden_copy.wait()
    pl.semaphore_wait(bar, 22)

    for dx, dc in FAR:
        send(hb.at[n], hf.at[n], 15, 1, (r, head_at(dx, 1, dc)))
    for dx, dc in NEAR:
        send(hb.at[n], hb.at[n], 0, 0, (r, head_at(dx, 0, dc)))

    copies[0].wait()
    copies[1].wait()
    for dzq in (2, 3, 1):
        pl.semaphore_signal(qsem, inc=1, device_id=(y * 8 + zt * 4 + zqs[dzq], h), device_id_type=MESH)
    for i in range(2, 20):
        copies[i].wait()
    gs[...] = jnp.broadcast_to(fgain_ref[...] * sw_ref[...], (8, 128))
    gb[zh] = gs[...]
    send(gs, gb.at[zh], 11, 20, (r, head_at(0, 1, 0)))

    prompt = gp_ref[r]
    plen = plen_ref[prompt]
    tails = [tlen_ref[i, prompt] for i in range(4)]

    def find(g, found):
        value = gp_ref[g]
        mine = jnp.where(value == r, g, found[8])
        return tuple(jnp.where(value == y * 8 + i, g, found[i]) for i in range(8)) + (mine,)

    owners = lax.fori_loop(0, 32, find, (jnp.int32(0),) * 9)

    row = lax.broadcasted_iota(jnp.int32, (8, 128), 0)
    lane = lax.broadcasted_iota(jnp.int32, (8, 128), 1)
    position = plen + row % 2
    for i in range(4):
        position = position + jnp.where(row // 2 == i, tails[i], 0)
    half_lane = (lane % 64).astype(F32)
    frequency = jnp.exp(-math.log(THETA) * 2.0 * half_lane / 128.0)
    angle = position.astype(F32) * frequency
    cosine = jnp.cos(angle)
    sine = jnp.sin(angle)
    sine = jnp.where(lane < 64, -sine, sine)

    def normed_rotated(value, gain):
        value = value * lax.rsqrt(jnp.mean(value * value, axis=-1, keepdims=True) + EPS) * gain
        return value * cosine + pltpu.roll(value, 64, 1) * sine

    def features(half, at):
        place = at * 4 + half * 2
        offset = pl.multiple_of(place * 128, 256)
        ref = hb if half is zh else hf
        value = jnp.concatenate([ref[at * 2].astype(F32), ref[at * 2 + 1].astype(F32)], axis=1)
        scaled = (value * again_ref[:, pl.ds(offset, 256)]).astype(BF)
        return value * value, scaled, offset

    kt[...] = kc[...].T
    wait_recv(hb.at[pl.ds(0, 7)], 0)
    squares = jnp.zeros((8, 256), F32)
    q_acc = jnp.zeros((8, 128), F32)
    g_acc = jnp.zeros((8, 128), F32)
    kv_acc = jnp.zeros((8, 128), F32)
    for i in range(4):
        square, scaled, offset = features(zh, i)
        squares = squares + square
        q_acc = q_acc + dot(scaled, wq[pl.ds(offset, 256), :])
        g_acc = g_acc + dot(scaled, wg[pl.ds(offset, 256), :])
        kv_acc = kv_acc + dot(scaled, wkv[pl.ds(offset, 256), :])
    wait_recv(hf, 1)
    rest = []
    for i in range(4):
        square, scaled, offset = features(oh, i)
        squares = squares + square
        rest.append((scaled, offset))
        q_acc = q_acc + dot(scaled, wq[pl.ds(offset, 256), :])
    row_scale = lax.rsqrt(jnp.sum(squares, axis=-1, keepdims=True) / WIDTH + EPS)
    query = normed_rotated(q_acc * row_scale, qgain_ref[...]).astype(BF)
    qs[...] = query
    qb[n] = query

    for dx, dc in FAR:
        send(qs, qf.at[n], 16, 3, (r, head_at(dx, 1, dc)))
    for dx, dc in NEAR:
        send(qs, qb.at[n], 1, 2, (r, head_at(dx, 0, dc)))

    send(wmlp.at[own_w], wfar, 13, 22, across)
    for dy in (2, 1, 3):
        send(wmlp.at[own_w], wmlp.at[own_w], 12, 21, (ys_[dy] * 8 + z, h))

    for scaled, offset in rest:
        g_acc = g_acc + dot(scaled, wg[pl.ds(offset, 256), :])
        kv_acc = kv_acc + dot(scaled, wkv[pl.ds(offset, 256), :])
    gate = jax.nn.sigmoid(g_acc * row_scale)
    projected = kv_acc * row_scale
    fresh = jnp.where(c == 0, normed_rotated(projected, kgain_ref[...]), projected).astype(BF)
    fs[...] = fresh
    fb[c] = fresh
    send(fs, fb.at[c], 2, 4, (r, head_at(0, 0, 1)))

    def attend(half, queries, sums):
        q = queries[...].astype(F32).reshape(64, 128).astype(BF)

        def weights(keys, live):
            scores = dot(q, keys) * SCALE
            rows = lax.broadcasted_iota(jnp.int32, scores.shape, 0)
            cols = lax.broadcasted_iota(jnp.int32, scores.shape, 1)
            seen = ((cols & 7) == (rows >> 4) * 2 + half) & live(rows, cols)
            return jnp.where(seen, jnp.exp(scores), 0.0)

        def tail_live(rows, cols):
            limit = jnp.where(cols < 256, jnp.where(cols < 128, tails[0], tails[1]),
                              jnp.where(cols < 384, tails[2], tails[3])) - h * 16
            return ((cols >> 7) == ((rows & 7) >> 1)) & (((cols >> 3) & 15) < limit)

        w_prefix = weights(kt[:, pl.ds(0, 2048)], lambda rows, cols: (cols >> 3) < plen - h * 256)
        w_tail = weights(kt[:, pl.ds(2048, 512)], tail_live)
        numer = dot(w_prefix.astype(BF), vc[pl.ds(0, 2048), :]) + dot(w_tail.astype(BF), vc[pl.ds(2048, 512), :])
        total = jnp.sum(w_prefix, axis=-1, keepdims=True) + jnp.sum(w_tail, axis=-1, keepdims=True)
        high = total.astype(BF).astype(F32)
        lanes = lax.broadcasted_iota(jnp.int32, (64, 128), 1)
        totals = jnp.where(lanes < 64, high, total - high)
        both = jnp.concatenate([numer.reshape(8, 8, 128), totals.reshape(8, 8, 128)], axis=1)
        sums[...] = both.astype(BF)

    wait_recv(qb.at[pl.ds(0, 7)], 2)
    attend(zh, qb, mb)
    nb[n] = mb[n]
    for dx, dc in NEAR:
        send(mb.at[near_at(dx, dc)], nb.at[n], 3, 5, (r, head_at(dx, 0, dc)))
    wait_recv(qf, 3)
    attend(oh, qf, mf)
    for dx, dc in FAR:
        send(mf.at[near_at(dx, dc)], nf.at[n], 17, 6, (r, head_at(dx, 1, dc)))

    wait_recv(wfar, 22)
    for dy in (2, 1, 3):
        send(wfar, wmlp.at[other_w], 8, 11, (ys_[dy] * 8 + z, h))
    kept = pltpu.make_async_copy(wfar, wmlp.at[other_w], lsem.at[21])
    kept.start()

    wait_recv(fb.at[0], 4)
    scores = dot_nt(query, fb[0]) * SCALE
    rows = lax.broadcasted_iota(jnp.int32, (8, 8), 0)
    cols = lax.broadcasted_iota(jnp.int32, (8, 8), 1)
    w_fresh = jnp.where((rows // 2 == cols // 2) & (cols <= rows), jnp.exp(scores), 0.0)
    numer = dot(w_fresh.astype(BF), fb[1])
    total = jnp.sum(w_fresh, axis=-1, keepdims=True)

    wait_recv(nb.at[pl.ds(0, 7)], 5)
    sums = jnp.sum(nb[...].astype(F32), axis=0)
    wait_recv(nf, 6)
    sums = sums + jnp.sum(nf[...].astype(F32), axis=0)
    numer = numer + sums[:8]
    total = total + sums[8:, 0:1] + sums[8:, 64:65]
    gated = (numer / total * gate).astype(BF)

    def quarter(low, high, odd):
        low = jnp.where(odd == 0, low, pltpu.roll(low, 64, 1))
        high = jnp.where(odd == 0, pltpu.roll(high, 64, 1), high)
        return jnp.where(lane < 64, low, high)

    mixed = dot(gated, wo[...])
    for place in range(8):
        px, pc = place // 2, place % 2
        for j in range(2):
            at = (2 * pc + j) * 512 + px * 64
            pieces = [mixed[:, at:at + 64], mixed[:, at + 256:at + 320]]
            sb[place, j] = jnp.concatenate(pieces, axis=1).astype(BF)
            block = 4 * px + 2 * j + pc
            sb[place, 2 + j] = mixed[:, block * 128:(block + 1) * 128].astype(BF)
    rb[n] = sb[n]
    for dx, dc in NEAR:
        send(sb.at[near_at(dx, dc)], rb.at[n], 4, 7, (r, head_at(dx, 0, dc)))
    wait_recv(rb.at[pl.ds(0, 7)], 7)
    sums = jnp.sum(rb[...].astype(F32), axis=0)
    first = jnp.where(zh == 0, 1.0, 0.0)

    for j in range(2):
        place = (2 * c + j) * 2 + lax.div(x, 2)
        tb[j] = (sums[j] + quarter(hb[place].astype(F32), hf[place].astype(F32), lax.rem(x, 2)) * first).astype(BF)
    residual = [sums[2] + hb[n].astype(F32) * first, sums[3] + hf[n].astype(F32) * first]

    slot = (zh * 4 + zq) * 2 + c
    target = y * 8 + zt * 4 + x
    pl.semaphore_wait(qsem, 3)
    for dz in (1, 0):
        for dx, dc in FAR:
            if dz or dx or dc:
                send(tb, xb.at[slot], 5, 8, (target, head_at(dx, dz, dc)))

    @pl.when(x != zq)
    def _():
        send(tb, xb.at[slot], 14, 8, (target, h))

        wait_recv(xb, 8)

    gains = []
    for fy in range(4):
        pair = []
        for i in range(2):
            offset = pl.multiple_of((fy * 4 + 2 * i + lax.div(zq, 2)) * 128, 128)
            pair.append(jnp.broadcast_to(mgain_ref[:, pl.ds(offset, 128)], (8, 128)))
        gains.append(quarter(*pair, lax.rem(zq, 2))[0:1])

    @pl.when(x == zq)
    def _():
        xb[slot] = tb[...]
        wait_recv(xb.at[pl.ds(0, 15)], 8)

    halves = xb[...].astype(F32)
    attended = halves[:8] + halves[8:]
    squares = jnp.zeros((32, 128), F32)
    parts = []
    for fy in range(4):
        block = jnp.concatenate([attended[i * 2 + fy // 2, fy % 2] for i in range(4)], axis=0)
        squares = squares + block * block
        parts.append((block * gains[fy]).astype(BF))
    mlp_in = jnp.concatenate(parts, axis=1)
    square = jnp.sum(squares, axis=-1, keepdims=True)
    high = square.astype(BF).astype(F32)
    lanes = lax.broadcasted_iota(jnp.int32, (32, 128), 1)
    square = jnp.where(lanes < 64, high, square - high)
    wait_recv(wmlp.at[pl.ds(0, 3)], 21)
    wait_recv(wmlp.at[pl.ds(0, 3)], 11)
    kept.wait()
    both = dot(mlp_in, wmlp[...].reshape(512, 768))

    for i in range(4):
        rows = slice(i * 8, i * 8 + 8)
        ps[i, :, 0:768] = both[rows].astype(BF)
        ps[i, :, 768:896] = square[rows].astype(BF)
    pb[zq] = ps[zq]
    for dzq in (2, 3, 1):
        to = zqs[dzq]
        send(ps.at[to], pb.at[zq], 6, 9, (y * 8 + zt * 4 + to, h))
    wait_recv(pb.at[pl.ds(0, 3)], 9)
    sums = jnp.sum(pb[...].astype(F32), axis=0)
    scale = lax.rsqrt((sums[:, 768:769] + sums[:, 832:833]) / WIDTH + EPS)
    act = (jax.nn.silu(sums[:, 0:384] * scale) * (sums[:, 384:768] * scale)).astype(BF)

    down = dot(act, wdown[...])
    for place in range(8):
        px, pc = place // 2, place % 2
        for j, block in enumerate((4 * px + pc, 4 * px + 2 + pc)):
            ds_[place, j] = down[:, block * 128:(block + 1) * 128].astype(BF)
    for j in range(2):
        ds_[n, j] = (ds_[n, j].astype(F32) + residual[j]).astype(BF)
    db[y * 8 + n] = ds_[n]
    for dy, dx, dc in SPREAD:
        send(ds_.at[near_at(dx, dc)], db.at[y * 8 + n], 7, 10, (ys_[dy] * 8 + z, head_at(dx, 0, dc)))
    wait_recv(db.at[pl.ds(0, 31)], 10)
    for i in range(4):
        yb[i] = jnp.sum(db[pl.ds(i * 8, 8)].astype(F32), axis=0).astype(BF)

    for i in range(8):
        zs[i] = yb[lax.div(owners[i], 8)]
    zb_[zh * 8 + z] = zs[z]
    for dz, dzl in RING:
        to = zls[dzl]
        send(zs.at[to], zb_.at[zh * 8 + z], 9, 12, (y * 8 + to, head_at(0, dz, 0)))
    wait_recv(zb_.at[pl.ds(0, 15)], 12)
    wait_recv(gb.at[0], 20)
    from_z = lax.rem(owners[8], 8)
    final = (zb_[from_z].astype(F32) + zb_[8 + from_z].astype(F32)).astype(BF).astype(F32)
    out_ref[...] = jnp.where(zh == 0, final[0], final[1]).astype(BF)

    cs[0] = final[0] * final[0] + final[1] * final[1]
    cs[1] = final[0] * gb[0] + final[1] * gb[1]
    cb[n] = cs[...]
    for dx, dc in NEAR:
        send(cs, cb.at[n], 10, 13, (r, head_at(dx, 0, dc)))
    wait_recv(cb.at[pl.ds(0, 7)], 13)
    sums = jnp.sum(jnp.sum(cb[...], axis=0), axis=-1, keepdims=True)
    score = sums[1] * lax.rsqrt(sums[0] / WIDTH + EPS)
    score_ref[...] = jnp.sum(jnp.where(row == lane, score, 0.0), axis=0, keepdims=True)

    wait_send(hb.at[pl.ds(0, 7)], 0)
    wait_send(hf, 15)
    wait_send(qb.at[pl.ds(0, 7)], 1)
    wait_send(qf, 16)
    wait_send(fb.at[0], 2)
    wait_send(nb.at[pl.ds(0, 7)], 3)
    wait_send(nf, 17)
    wait_send(rb.at[pl.ds(0, 7)], 4)
    wait_send(xb.at[pl.ds(0, 15)], 5)

    @pl.when(x != zq)
    def _():
        wait_send(xb.at[0], 14)
    wait_send(pb.at[pl.ds(0, 3)], 6)
    wait_send(db.at[pl.ds(0, 31)], 7)
    wait_send(zb_.at[pl.ds(0, 15)], 9)
    wait_send(cb.at[pl.ds(0, 7)], 10)
    wait_send(gb.at[0], 11)
    wait_send(wmlp.at[pl.ds(0, 3)], 12)
    wait_send(wmlp.at[0], 13)
    wait_send(wmlp.at[pl.ds(0, 3)], 8)


def shards(
    hidden, attn_gain, q_weight, gate_weight, key_value_weight, q_gain, k_gain, out_weight,
    prompt_key_cache, prompt_value_cache, tail_key_cache, tail_value_cache, mlp_gain, mlp_gate,
    mlp_up, mlp_down, final_gain, score_weight, prompt_lengths, tail_lengths, group_prompt,
):
    vmem = pl.BlockSpec(memory_space=pltpu.VMEM)
    hbm = pl.BlockSpec(memory_space=pl.ANY)

    def blocks(*shape, kind=BF):
        return pltpu.VMEM(shape, kind)

    out, score = pl.pallas_call(
        kernel,
        out_shape=(pltpu.VMEM((8, 128), BF), pltpu.VMEM((1, 128), F32)),
        in_specs=[hbm] * 21,
        out_specs=(vmem, vmem),
        scratch_shapes=[
            pltpu.SMEM((32,), jnp.int32), pltpu.SMEM((4, 32), jnp.int32), pltpu.SMEM((32,), jnp.int32),
            blocks(1, 2048, kind=F32), blocks(1, 128, kind=F32), blocks(1, 128, kind=F32),
            blocks(1, 2048, kind=F32), blocks(1, 128, kind=F32), blocks(1, 128, kind=F32),
            blocks(2048, 128), blocks(2048, 128), blocks(2048, 128), blocks(128, 2048),
            blocks(2560, 128), blocks(128, 2560), blocks(2560, 128),
            blocks(8, 64, 768), blocks(64, 768), blocks(384, 2048),
            blocks(8, 8, 128), blocks(8, 8, 128),
            blocks(8, 128), blocks(8, 8, 128), blocks(8, 8, 128),
            blocks(8, 128), blocks(2, 8, 128),
            blocks(8, 16, 128), blocks(8, 16, 128),
            blocks(8, 16, 128), blocks(8, 16, 128),
            blocks(8, 4, 8, 128), blocks(8, 4, 8, 128),
            blocks(2, 8, 128), blocks(16, 2, 8, 128),
            blocks(4, 8, 896), blocks(4, 8, 896),
            blocks(8, 2, 8, 128), blocks(32, 2, 8, 128),
            blocks(4, 2, 8, 128),
            blocks(8, 2, 8, 128), blocks(16, 2, 8, 128),
            blocks(2, 8, 128, kind=F32), blocks(8, 2, 8, 128, kind=F32),
            blocks(8, 128, kind=F32), blocks(2, 8, 128, kind=F32),
            pltpu.SemaphoreType.DMA((22,)),
            pltpu.SemaphoreType.DMA((18,)),
            pltpu.SemaphoreType.DMA((23,)),
            pltpu.SemaphoreType.REGULAR,
        ],
        compiler_params=pltpu.CompilerParams(
            collective_id=0, has_side_effects=True, vmem_limit_bytes=60 << 20
        ),
    )(
        prompt_lengths, tail_lengths.T, group_prompt,
        hidden, attn_gain.reshape(1, -1), q_gain.reshape(1, -1), k_gain.reshape(1, -1),
        mlp_gain.reshape(1, -1), final_gain.reshape(1, -1), score_weight.reshape(1, -1),
        q_weight, gate_weight, key_value_weight, out_weight,
        prompt_key_cache.reshape(-1, 128), prompt_value_cache.reshape(-1, 128),
        tail_key_cache.reshape(-1, 128), tail_value_cache.reshape(-1, 128),
        mlp_gate, mlp_up, mlp_down,
    )
    return out, score[0, :8]


def solution(mesh):
    return jax.shard_map(
        shards,
        mesh=mesh,
        in_specs=(
            P("req", "head"),
            P(),
            P(None, "head"),
            P(None, "head"),
            P(None, "head"),
            P(),
            P(),
            P("head", None),
            P("req", "head", None, None),
            P("req", "head", None, None),
            P("req", None, "head", None, None),
            P("req", None, "head", None, None),
            P(),
            P("req", "head"),
            P("req", "head"),
            P("head", None),
            P("head"),
            P("head"),
            P(),
            P(),
            P(),
        ),
        out_specs=(P("req", "head"), P("req")),
        check_vma=False,
    )
```
